256 devices in a mesh: dp: 4 (over y_lo, core), row: 16 (over z, y_hi), col: 4 (over x).
Axes of the slice: x: 4, y: 4 (y_hi: 2, y_lo: 2; y = y_hi * 2 + y_lo), z: 8, core: 2. Of those that a mesh axis runs over, the one named last changes fastest.
Arguments:
- pair_act: bfloat16 [1024, 256, 128], P(('dp', 'row'), 'col'), parts along dimension 0, may hold values from -6 to 6
- gain_in: float32 [128], replicated, may hold values from 0.5 to 1.5
- bias_in: float32 [128], replicated, may hold values from -3 to 3
- proj_a: bfloat16 [1024, 256, 128], P(('dp', 'row'), 'col'), parts along dimension 0, may hold values from -6 to 6
- gate_a: bfloat16 [1024, 256, 128], P(('dp', 'row'), 'col'), parts along dimension 0, may hold values from -8 to 8
- proj_b: bfloat16 [1024, 256, 128], P(('dp', 'row'), 'col'), parts along dimension 0, may hold values from -6 to 6
- gate_b: bfloat16 [1024, 256, 128], P(('dp', 'row'), 'col'), parts along dimension 0, may hold values from -8 to 8
- tri_out: bfloat16 [1024, 256, 128], P(('dp', 'row'), 'col'), parts along dimension 0, may hold values from -12 to 12
- gain_tri: float32 [128], replicated, may hold values from 0.5 to 1.5
- bias_tri: float32 [128], replicated, may hold values from -3 to 3
- gate_out: bfloat16 [1024, 256, 128], P(('dp', 'row'), 'col'), parts along dimension 0, may hold values from -8 to 8
- cotangent: bfloat16 [1024, 256, 128], P(('dp', 'row'), 'col'), parts along dimension 0, may hold values from -6 to 6
- w_proj_a: bfloat16 [128, 128], replicated, may hold values from -0.5 to 0.5
- w_gate_a: bfloat16 [128, 128], replicated, may hold values from -0.5 to 0.5
- w_proj_b: bfloat16 [128, 128], replicated, may hold values from -0.5 to 0.5
- w_gate_b: bfloat16 [128, 128], replicated, may hold values from -0.5 to 0.5
- w_out: bfloat16 [128, 128], replicated, may hold values from -0.5 to 0.5
- w_gate: bfloat16 [128, 128], replicated, may hold values from -0.5 to 0.5
Outputs:
- pair_grad: bfloat16 [1024, 256, 128], P(('dp', 'row'), 'col'), parts along dimension 0
- gain_in_grad: float32 [512], P('dp'), parts along dimension 0
- bias_in_grad: float32 [512], P('dp'), parts along dimension 0
- gain_tri_grad: float32 [512], P('dp'), parts along dimension 0
- bias_tri_grad: float32 [512], P('dp'), parts along dimension 0
- w_proj_a_grad: float32 [512, 128], P('dp'), parts along dimension 0
- w_gate_a_grad: float32 [512, 128], P('dp'), parts along dimension 0
- w_proj_b_grad: float32 [512, 128], P('dp'), parts along dimension 0
- w_gate_b_grad: float32 [512, 128], P('dp'), parts along dimension 0
- w_out_grad: float32 [512, 128], P('dp'), parts along dimension 0
- w_gate_grad: float32 [512, 128], P('dp'), parts along dimension 0
The draws below stay inside these ranges and needn't reach their ends.
There are 4 independent parts, one for each index of `dp`. The reference program is written for one: setup_inputs(seed, part) draws one part's arguments, and reference() takes and returns one part's arrays. A program takes and returns all parts, laid end to end along the dimension named above; an argument that names none is the same for every part. Nothing has to cross between parts.
All inputs are finite; a program needn't handle non-finite values.
Results may differ from the reference program's by a relative error of at most 0.0072.
Values may be sent and summed in bfloat16 or wider, within the bound.
A program may use at most 128 MiB of HBM per device.

```python
import jax
import jax.numpy as jnp
from jax import lax

C = 128
H = 128
N = 256


def steps_of(rng, shape, cuts, low, largest):
    level, own = 1.0, jax.random.fold_in(rng, 6)
    for position, blocks in cuts:
        draws = jnp.exp(jax.random.uniform(jax.random.fold_in(own, position), (blocks,), jnp.float32, low / len(cuts), largest / len(cuts)))
        level = level * jnp.repeat(draws, shape[position] // blocks).reshape([-1 if axis == position else 1 for axis in range(len(shape))])
    return level


def normal_values(rng, dims, scale, reach, split=(), held_as=jnp.bfloat16):
    array = scale * jax.random.normal(rng, dims, jnp.float32)
    if split:
        array = array * steps_of(rng, dims, split, -0.22, 0.18)
    return jnp.clip(array, -reach, reach).astype(held_as)


def setup_inputs(seed: int = 0, part: int = 0) -> dict:
    key_of = jax.random.split(jax.random.key(seed), 19)
    part_splits = jax.random.split(jax.random.fold_in(key_of[18], part), 19)
    return {
        "pair_act": normal_values(part_splits[0], (N, N, C), 1.0, 6.0, ((0, 16), (1, 4))),
        "gain_in": jnp.clip(1.0 + 0.1 * jax.random.normal(key_of[1], (C,), jnp.float32), 0.5, 1.5),
        "bias_in": normal_values(key_of[2], (C,), 0.5, 3.0, (), jnp.float32),
        "proj_a": normal_values(part_splits[3], (N, N, H), 1.0, 6.0, ((0, 16), (1, 4))),
        "gate_a": normal_values(part_splits[4], (N, N, H), 1.5, 8.0, ((0, 16), (1, 4))),
        "proj_b": normal_values(part_splits[5], (N, N, H), 1.0, 6.0, ((0, 16), (1, 4))),
        "gate_b": normal_values(part_splits[6], (N, N, H), 1.5, 8.0, ((0, 16), (1, 4))),
        "tri_out": normal_values(part_splits[7], (N, N, H), 2.0, 12.0, ((0, 16), (1, 4))),
        "gain_tri": jnp.clip(1.0 + 0.1 * jax.random.normal(key_of[8], (H,), jnp.float32), 0.5, 1.5),
        "bias_tri": normal_values(key_of[9], (H,), 0.5, 3.0, (), jnp.float32),
        "gate_out": normal_values(part_splits[10], (N, N, C), 1.5, 8.0, ((0, 16), (1, 4))),
        "cotangent": normal_values(part_splits[11], (N, N, C), 1.0, 6.0, ((0, 16), (1, 4))),
        "w_proj_a": normal_values(key_of[12], (C, H), C ** -0.5, 0.5),
        "w_gate_a": normal_values(key_of[13], (C, H), C ** -0.5, 0.5),
        "w_proj_b": normal_values(key_of[14], (C, H), C ** -0.5, 0.5),
        "w_gate_b": normal_values(key_of[15], (C, H), C ** -0.5, 0.5),
        "w_out": normal_values(key_of[16], (H, C), H ** -0.5, 0.5),
        "w_gate": normal_values(key_of[17], (C, C), C ** -0.5, 0.5),
    }


def normalize(values):
    average = lax.optimization_barrier(jnp.mean(values, axis=-1, keepdims=True))
    centred = values - average
    inverse = lax.rsqrt(lax.optimization_barrier(jnp.mean(centred * centred, axis=-1, keepdims=True)) + 1e-05)
    return (centred * inverse, inverse)

def norm_back(grad_hat, normed, inverse):
    grad_mean = lax.optimization_barrier(jnp.mean(grad_hat, axis=-1, keepdims=True))
    grad_corr = lax.optimization_barrier(jnp.mean(grad_hat * normed, axis=-1, keepdims=True))
    return inverse * (grad_hat - grad_mean - normed * grad_corr)

def outer_sum(left_mat, right_mat):
    return jnp.dot(left_mat.T, right_mat, preferred_element_type=jnp.float32)

def reference(pair_act, gain_in, bias_in, proj_a, gate_a, proj_b, gate_b, tri_out, gain_tri, bias_tri, gate_out, cotangent, w_proj_a, w_gate_a, w_proj_b, w_gate_b, w_out, w_gate):
    feature = pair_act.shape[2]
    hidden_w = tri_out.shape[2]
    normed, inverse = normalize(pair_act.astype(jnp.float32))
    pair_normed = (normed * gain_in + bias_in).astype(jnp.bfloat16)
    flat_normed = pair_normed.reshape(-1, feature)
    sig_a = jax.nn.sigmoid(gate_a.astype(jnp.float32))
    sig_b = jax.nn.sigmoid(gate_b.astype(jnp.float32))
    left_act = (sig_a * proj_a.astype(jnp.float32)).astype(jnp.bfloat16)
    right_act = (sig_b * proj_b.astype(jnp.float32)).astype(jnp.bfloat16)
    tri_hat, tri_inverse = normalize(tri_out.astype(jnp.float32))
    mixed_tri = (tri_hat * gain_tri + bias_tri).astype(jnp.bfloat16).reshape(-1, hidden_w)
    lifted = jnp.dot(mixed_tri, w_out, preferred_element_type=jnp.float32)
    sig_out = jax.nn.sigmoid(gate_out.astype(jnp.float32)).reshape(-1, feature)
    upstream = cotangent.astype(jnp.float32).reshape(-1, feature)
    grad_lift = (upstream * sig_out).astype(jnp.bfloat16)
    grad_gate = (upstream * lifted * sig_out * (1.0 - sig_out)).astype(jnp.bfloat16)
    grad_mixed = jnp.dot(grad_lift, w_out.T, preferred_element_type=jnp.float32)
    w_out_grad = outer_sum(mixed_tri, grad_lift)
    w_gate_grad = outer_sum(flat_normed, grad_gate)
    flat_hat = tri_hat.reshape(-1, hidden_w)
    gain_tri_grad = lax.optimization_barrier(jnp.sum(grad_mixed * flat_hat, axis=0))
    bias_tri_grad = lax.optimization_barrier(jnp.sum(grad_mixed, axis=0))
    grad_mixed = grad_mixed.reshape(tri_out.shape)
    grad_tri = norm_back(grad_mixed * gain_tri, tri_hat, tri_inverse).astype(jnp.bfloat16)
    grad_wide = grad_tri.astype(jnp.float32)
    d_left = jnp.einsum('ijc,jkc->ikc', grad_wide, right_act.astype(jnp.float32))
    d_right = jnp.einsum('ijc,ikc->jkc', grad_wide, left_act.astype(jnp.float32))
    grad_pa = (d_left * sig_a).astype(jnp.bfloat16).reshape(-1, hidden_w)
    grad_ga = (d_left * proj_a.astype(jnp.float32) * sig_a * (1.0 - sig_a)).astype(jnp.bfloat16).reshape(-1, hidden_w)
    grad_pb = (d_right * sig_b).astype(jnp.bfloat16).reshape(-1, hidden_w)
    grad_gb = (d_right * proj_b.astype(jnp.float32) * sig_b * (1.0 - sig_b)).astype(jnp.bfloat16).reshape(-1, hidden_w)
    grad_normed = jnp.dot(grad_pa, w_proj_a.T, preferred_element_type=jnp.float32)
    grad_normed = grad_normed + jnp.dot(grad_ga, w_gate_a.T, preferred_element_type=jnp.float32)
    grad_normed = grad_normed + jnp.dot(grad_pb, w_proj_b.T, preferred_element_type=jnp.float32)
    grad_normed = grad_normed + jnp.dot(grad_gb, w_gate_b.T, preferred_element_type=jnp.float32)
    grad_normed = grad_normed + jnp.dot(grad_gate, w_gate.T, preferred_element_type=jnp.float32)
    w_proj_a_grad = outer_sum(flat_normed, grad_pa)
    w_gate_a_grad = outer_sum(flat_normed, grad_ga)
    w_proj_b_grad = outer_sum(flat_normed, grad_pb)
    w_gate_b_grad = outer_sum(flat_normed, grad_gb)
    flat_plain = normed.reshape(-1, feature)
    gain_in_grad = lax.optimization_barrier(jnp.sum(grad_normed * flat_plain, axis=0))
    bias_in_grad = lax.optimization_barrier(jnp.sum(grad_normed, axis=0))
    grad_normed = grad_normed.reshape(pair_act.shape)
    pair_grad = norm_back(grad_normed * gain_in, normed, inverse).astype(jnp.bfloat16)
    return (pair_grad, gain_in_grad, bias_in_grad, gain_tri_grad, bias_tri_grad, w_proj_a_grad, w_gate_a_grad, w_proj_b_grad, w_gate_b_grad, w_out_grad, w_gate_grad)
```

```python
import jax
import jax.numpy as jnp
from jax import lax
from jax.experimental import pallas as pl
from jax.experimental.pallas import tpu as pltpu
from jax.sharding import PartitionSpec as P

MESH = pl.DeviceIdType.MESH
F32 = jnp.float32
BF16 = jnp.bfloat16
ROWS = 16
COLS = 4
GROUP = ROWS * COLS
TI = 16
TJ = 64
CELLS = TI * TJ
CH = 128
STEP = 2
TURNS = TI // STEP
SPAN = STEP * TJ


def dot(a, b):
    return jnp.dot(a, b, preferred_element_type=F32)


def dot_nt(a, b):
    return lax.dot_general(a, b, (((1,), (1,)), ((), ())), preferred_element_type=F32)


def dot_tn(a, b):
    return lax.dot_general(a, b, (((0,), (0,)), ((), ())), preferred_element_type=F32)


def sigmoid(x):
    return 1.0 / (1.0 + jnp.exp(-x))


def normalize(values):
    average = jnp.mean(values, axis=-1, keepdims=True)
    centred = values - average
    inverse = lax.rsqrt(jnp.mean(centred * centred, axis=-1, keepdims=True) + 1e-05)
    return centred * inverse, inverse


def norm_back(grad_hat, normed, inverse):
    grad_mean = jnp.mean(grad_hat, axis=-1, keepdims=True)
    grad_corr = jnp.mean(grad_hat * normed, axis=-1, keepdims=True)
    return inverse * (grad_hat - grad_mean - normed * grad_corr)


def fold_rows(x):
    return jnp.sum(x.reshape(-1, 8, CH), axis=0)


def kernel(
    pair_act, proj_a, gate_a, proj_b, gate_b, tri_out, gate_out, cotangent,
    gain_in, bias_in, gain_tri, bias_tri,
    w_proj_a, w_gate_a, w_proj_b, w_gate_b, w_out, w_gate,
    pair_grad, vec_out, w_pa_g, w_ga_g, w_pb_g, w_gb_g, w_out_g, w_gate_g,
    tmp, tmp2, left_t, right_t, grad_t, left_r, right_r, grad_r,
    dl_s, dr_s, dl_r, dr_r, rbd,
    sig_a, sig_b, mixed_s, lift_s, ggate_s, normed_s, inv_s, pn_s, gn_s, ga1, ga2,
    part, part_r, total, final, vec_acc,
    send, recv,
):
    d, r, c = lax.axis_index("dp"), lax.axis_index("row"), lax.axis_index("col")
    mine = r * COLS + c

    def peer_of(k):
        return lax.rem(r + k // COLS, ROWS), lax.rem(c + lax.rem(k, COLS), COLS)

    barrier = pltpu.get_barrier_semaphore()

    def greet(k, _):
        pr, pc = peer_of(k)
        pl.semaphore_signal(barrier, inc=1, device_id=(d, pr, pc), device_id_type=MESH)
        return 0

    lax.fori_loop(1, GROUP, greet, 0)

    lane = lax.broadcasted_iota(jnp.int32, (TJ, CH), 1)
    low = lane < TJ
    row = lax.broadcasted_iota(jnp.int32, (TJ, CH), 0)
    fold = jnp.where(lax.rem(lane, TJ) == row, 1.0, 0.0).astype(BF16)

    def halves(x):
        zero = jnp.zeros_like(x)
        return jnp.concatenate([jnp.where(low, x, zero), jnp.where(low, zero, x)], axis=0)

    def turned(blocks):
        return dot_nt(fold, jnp.concatenate([halves(b) for b in blocks], axis=0).astype(BF16))

    def spread(scratch, s, flat):
        out = turned([flat[h * TJ : (h + 1) * TJ] for h in range(STEP)])
        for h in range(STEP):
            scratch[pl.ds(s * STEP + h, GROUP, stride=TI), :] = out[:, h * CH : (h + 1) * CH]

    def acts(s, _):
        at = pl.ds(s * STEP, STEP)
        for gate, proj, sig, scratch in ((gate_b, proj_b, sig_b, tmp), (gate_a, proj_a, sig_a, tmp2)):
            sg = sigmoid(gate[at].reshape(SPAN, CH).astype(F32))
            sig[pl.ds(s * SPAN, SPAN), :] = sg
            act = sg * proj[at].reshape(SPAN, CH).astype(F32)
            spread(scratch, s, act.astype(BF16).astype(F32))
        return 0

    lax.fori_loop(0, TURNS, acts, 0)
    right_t[...] = tmp[...].astype(BF16).reshape(GROUP, TI, CH)
    left_t[...] = tmp2[...].astype(BF16).reshape(GROUP, TI, CH)

    pl.semaphore_wait(barrier, GROUP - 1)

    def scatter(source, target, n):
        def go(k, _):
            pr, pc = peer_of(k)
            pltpu.make_async_remote_copy(
                src_ref=source.at[pr * COLS + pc], dst_ref=target.at[c, r],
                send_sem=send.at[n], recv_sem=recv.at[n],
                device_id=(d, pr, pc), device_id_type=MESH,
            ).start()
            return 0

        lax.fori_loop(1, GROUP, go, 0)
        target[c, r] = source[mine]

    def scatter_back(source, target, n):
        def go(k, _):
            pr, pc = peer_of(k)
            pltpu.make_async_remote_copy(
                src_ref=source.at[pc, pr], dst_ref=target.at[mine],
                send_sem=send.at[n], recv_sem=recv.at[n],
                device_id=(d, pr, pc), device_id_type=MESH,
            ).start()
            return 0

        lax.fori_loop(1, GROUP, go, 0)
        target[mine] = source[c, r]

    def arrived(n, like):
        view = like.at[pl.ds(0, GROUP - 1)]
        pltpu.make_async_copy(view, view, recv.at[n]).wait()

    def left_here(n, like):
        view = like.at[pl.ds(0, GROUP - 1)]
        pltpu.make_async_copy(view, view, send.at[n]).wait()

    scatter(right_t, right_r, 0)
    scatter(left_t, left_r, 1)

    g_tri, b_tri = gain_tri[...], bias_tri[...]
    vec_acc[...] = jnp.zeros_like(vec_acc)

    def outer(s, _):
        at, cells = pl.ds(s * STEP, STEP), pl.ds(s * SPAN, SPAN)
        hat, inv = normalize(tri_out[at].reshape(SPAN, CH).astype(F32))
        mixed = (hat * g_tri + b_tri).astype(BF16)
        lifted = dot(mixed, w_out[...])
        sg = sigmoid(gate_out[at].reshape(SPAN, CH).astype(F32))
        up = cotangent[at].reshape(SPAN, CH).astype(F32)
        ups = up * sg
        lift = ups.astype(BF16)
        ggate_s[cells, :] = (ups * lifted * (1.0 - sg)).astype(BF16)
        mixed_s[cells, :] = mixed
        lift_s[cells, :] = lift
        gm = dot_nt(lift, w_out[...])
        vec_acc[0] += fold_rows(gm * hat)
        vec_acc[1] += fold_rows(gm)
        gt = norm_back(gm * g_tri, hat, inv)
        spread(tmp, s, gt.astype(BF16).astype(F32))
        return 0

    lax.fori_loop(0, TURNS, outer, 0)
    grad_t[...] = tmp[...].astype(BF16).reshape(GROUP, TI, CH)
    scatter(grad_t, grad_r, 2)

    g_in, b_in = gain_in[...], bias_in[...]

    def first(s, _):
        at, cells = pl.ds(s * STEP, STEP), pl.ds(s * SPAN, SPAN)
        normed, inv = normalize(pair_act[at].reshape(SPAN, CH).astype(F32))
        normed_s[cells, :] = normed
        inv_s[cells, :] = jnp.broadcast_to(inv, (SPAN, CH))
        pn_s[cells, :] = (normed * g_in + b_in).astype(BF16)
        gn_s[cells, :] = dot_nt(ggate_s[cells, :], w_gate[...])
        return 0

    lax.fori_loop(0, TURNS, first, 0)
    part[:, 8:12, :] = jnp.concatenate(
        [dot_tn(mixed_s[...], lift_s[...]), dot_tn(pn_s[...], ggate_s[...])], axis=0
    ).reshape(GROUP, 4, CH)

    arrived(0, right_t)
    arrived(1, left_t)
    arrived(2, grad_t)
    for k in range(COLS):
        for j in range(COLS):
            tile = right_r[k, 4 * j : 4 * j + 4].reshape(TJ, CH)
            rbd[j * CH : (j + 1) * CH, k * CH : (k + 1) * CH] = halves(tile.astype(F32)).astype(BF16)
    grads = jnp.concatenate([grad_r[k].reshape(ROWS * TI, CH) for k in range(COLS)], axis=1)
    lefts = jnp.concatenate([left_r[k].reshape(ROWS * TI, CH) for k in range(COLS)], axis=1)
    d_left = dot(grads, rbd[...]).astype(BF16)
    for k in range(COLS):
        dl_s[k] = d_left[:, k * CH : (k + 1) * CH].reshape(ROWS, TI, CH)
    scatter_back(dl_s, dl_r, 3)
    d_right = dot_tn(grads, lefts)
    for k in range(COLS):
        for j in range(COLS):
            tile = d_right[j * CH : (j + 1) * CH, k * CH : (k + 1) * CH]
            dr_s[k, 4 * j : 4 * j + 4] = (
                jnp.where(low, tile[:TJ], tile[TJ:]).astype(BF16).reshape(4, TI, CH)
            )
    scatter_back(dr_s, dr_r, 4)

    def side(arr, n, like, sig, proj, wp, wg, base):
        arrived(n, like)
        tmp[...] = arr[...].reshape(CELLS, CH).astype(F32)

        def go(s, _):
            at, cells = pl.ds(s * STEP, STEP), pl.ds(s * SPAN, SPAN)
            blocks = [tmp[pl.ds(s * STEP + h, GROUP, stride=TI), :] for h in range(STEP)]
            out = turned(blocks)
            dd = jnp.concatenate([out[:, h * CH : (h + 1) * CH] for h in range(STEP)], axis=0)
            sg = sig[cells, :]
            ds = dd * sg
            gp = ds.astype(BF16)
            gg = (ds * proj[at].reshape(SPAN, CH).astype(F32) * (1.0 - sg)).astype(BF16)
            ga1[cells, :] = gp
            ga2[cells, :] = gg
            gn_s[cells, :] += dot_nt(gp, wp[...]) + dot_nt(gg, wg[...])
            return 0

        lax.fori_loop(0, TURNS, go, 0)
        part[base : base + 16, 0:8, :] = dot_tn(pn_s[...], ga1[...]).reshape(16, 8, CH)
        part[base + 16 : base + 32, 0:8, :] = dot_tn(pn_s[...], ga2[...]).reshape(16, 8, CH)

    side(dl_r, 3, dl_s_like(right_t), sig_a, proj_a, w_proj_a, w_gate_a, 0)
    side(dr_r, 4, dl_s_like(right_t), sig_b, proj_b, w_proj_b, w_gate_b, 32)

    def last(s, _):
        at, cells = pl.ds(s * STEP, STEP), pl.ds(s * SPAN, SPAN)
        gn, normed = gn_s[cells, :], normed_s[cells, :]
        vec_acc[2] += fold_rows(gn * normed)
        vec_acc[3] += fold_rows(gn)
        back = norm_back(gn * g_in, normed, inv_s[cells, :])
        pair_grad[at] = back.astype(BF16).reshape(STEP, TJ, CH)
        return 0

    lax.fori_loop(0, TURNS, last, 0)
    vecs = jnp.concatenate([jnp.sum(vec_acc[n], axis=0, keepdims=True) for n in range(4)], axis=0)
    part[:, 12:16, :] = jnp.broadcast_to(vecs[None], (GROUP, 4, CH))

    def reduce_go(k, _):
        pr, pc = peer_of(k)
        pltpu.make_async_remote_copy(
            src_ref=part.at[pr * COLS + pc], dst_ref=part_r.at[mine],
            send_sem=send.at[5], recv_sem=recv.at[5],
            device_id=(d, pr, pc), device_id_type=MESH,
        ).start()
        return 0

    lax.fori_loop(1, GROUP, reduce_go, 0)
    part_r[mine] = part[mine]
    arrived(5, part)
    total[...] = jnp.sum(part_r[...], axis=0)

    def gather_go(k, _):
        pr, pc = peer_of(k)
        pltpu.make_async_remote_copy(
            src_ref=total, dst_ref=final.at[mine],
            send_sem=send.at[6], recv_sem=recv.at[6],
            device_id=(d, pr, pc), device_id_type=MESH,
        ).start()
        return 0

    lax.fori_loop(1, GROUP, gather_go, 0)
    final[mine] = total[...]
    vec_out[...] = total[12:16, :]
    arrived(6, part)
    for n, ref in enumerate((w_pa_g, w_ga_g, w_pb_g, w_gb_g)):
        ref[...] = final[16 * n : 16 * n + 16, 0:8, :].reshape(CH, CH)
    both = final[:, 8:12, :].reshape(2 * CH, CH)
    w_out_g[...] = both[:CH]
    w_gate_g[...] = both[CH:]
    for n in range(5):
        left_here(n, right_t)
    left_here(5, part)
    left_here(6, part)


def dl_s_like(ref):
    return ref


def local(
    pair_act, gain_in, bias_in, proj_a, gate_a, proj_b, gate_b, tri_out, gain_tri, bias_tri,
    gate_out, cotangent, w_proj_a, w_gate_a, w_proj_b, w_gate_b, w_out, w_gate,
):
    vmem = pl.BlockSpec(memory_space=pltpu.VMEM)
    square = jax.ShapeDtypeStruct((CH, CH), F32)
    turned = pltpu.VMEM((GROUP, TI, CH), BF16)
    landed = pltpu.VMEM((COLS, ROWS, TI, CH), BF16)
    wide = pltpu.VMEM((CELLS, CH), F32)
    half = pltpu.VMEM((CELLS, CH), BF16)
    outs = pl.pallas_call(
        kernel,
        out_shape=(
            jax.ShapeDtypeStruct(pair_act.shape, BF16),
            jax.ShapeDtypeStruct((4, CH), F32),
            square, square, square, square, square, square,
        ),
        in_specs=[vmem] * 18,
        out_specs=tuple([vmem] * 8),
        scratch_shapes=[
            wide, wide, turned, turned, turned, landed, landed, landed,
            landed, landed, turned, turned, pltpu.VMEM((4 * CH, 4 * CH), BF16),
            wide, wide, half, half, half, wide, wide, half, wide, half, half,
            pltpu.VMEM((GROUP, 16, CH), F32), pltpu.VMEM((GROUP, 16, CH), F32),
            pltpu.VMEM((16, CH), F32), pltpu.VMEM((GROUP, 16, CH), F32), pltpu.VMEM((4, 8, CH), F32),
            pltpu.SemaphoreType.DMA((7,)), pltpu.SemaphoreType.DMA((7,)),
        ],
        compiler_params=pltpu.CompilerParams(
            collective_id=0, has_side_effects=True, vmem_limit_bytes=48 * 1024 * 1024
        ),
        name="triangle_backward",
    )(
        pair_act, proj_a, gate_a, proj_b, gate_b, tri_out, gate_out, cotangent,
        gain_in.reshape(1, CH), bias_in.reshape(1, CH), gain_tri.reshape(1, CH), bias_tri.reshape(1, CH),
        w_proj_a, w_gate_a, w_proj_b, w_gate_b, w_out, w_gate,
    )
    pair_grad, vecs, w_pa, w_ga, w_pb, w_gb, w_o, w_g = outs
    return (pair_grad, vecs[2], vecs[3], vecs[0], vecs[1], w_pa, w_ga, w_pb, w_gb, w_o, w_g)


def solution(mesh):
    tile = P(("dp", "row"), "col", None)
    placed = (
        tile, P(), P(), tile, tile, tile, tile, tile, P(), P(),
        tile, tile, P(), P(), P(), P(), P(), P(),
    )
    vector, matrix = P("dp"), P("dp", None)
    return jax.shard_map(
        local,
        mesh=mesh,
        in_specs=placed,
        out_specs=(tile,) + (vector,) * 4 + (matrix,) * 6,
        check_vma=False,
    )
```

```python
import jax
import jax.numpy as jnp
from jax import lax
from jax.experimental import pallas as pl
from jax.experimental.pallas import tpu as pltpu
from jax.sharding import PartitionSpec as P

MESH = pl.DeviceIdType.MESH
F32 = jnp.float32
BF16 = jnp.bfloat16
ROWS = 16
COLS = 4
GROUP = ROWS * COLS
TI = 16
TJ = 64
CELLS = TI * TJ
CH = 128
STEP = 2
TURNS = TI // STEP
SPAN = STEP * TJ
SUMMERS = GROUP // 2
BIG = 8


def dot(a, b):
    return jnp.dot(a, b, preferred_element_type=F32)


def dot_nt(a, b):
    return lax.dot_general(a, b, (((1,), (1,)), ((), ())), preferred_element_type=F32)


def dot_tn(a, b):
    return lax.dot_general(a, b, (((0,), (0,)), ((), ())), preferred_element_type=F32)


def sigmoid(x):
    return 1.0 / (1.0 + jnp.exp(-x))


def normalize(values):
    average = jnp.mean(values, axis=-1, keepdims=True)
    centred = values - average
    inverse = lax.rsqrt(jnp.mean(centred * centred, axis=-1, keepdims=True) + 1e-05)
    return centred * inverse, inverse


def norm_back(grad_hat, normed, inverse):
    grad_mean = jnp.mean(grad_hat, axis=-1, keepdims=True)
    grad_corr = jnp.mean(grad_hat * normed, axis=-1, keepdims=True)
    return inverse * (grad_hat - grad_mean - normed * grad_corr)


def fold_rows(x):
    return jnp.sum(x.reshape(-1, 8, CH), axis=0)


def kernel(*refs):
    hbm_in, refs = refs[:18], refs[18:]
    (pair_o, vec_o, *w_o), refs = refs[:8], refs[8:]
    held, refs = refs[:18], refs[18:]
    (pair_act, proj_a, gate_a, proj_b, gate_b, tri_out, gate_out, cotangent,
     gain_in, bias_in, gain_tri, bias_tri,
     w_proj_a, w_gate_a, w_proj_b, w_gate_b, w_out, w_gate) = held
    (tmp, tmp2, left_t, right_t, grad_t, left_r, right_r, grad_r,
     dl_s, dr_s, dl_r, dr_r, rbd,
     sig_a, sig_b, mixed_s, lift_s, ggate_s, normed_s, inv_s, pn_s, pn_t, gn_s, gpg_s, w_a, w_b,
     part, part_r, final, vec_acc, vec_s, vec_r, vec_c, vec_a,
     in_sem, send, recv) = refs
    d, r, c = lax.axis_index("dp"), lax.axis_index("row"), lax.axis_index("col")
    mine = r * COLS + c

    fetches = [pltpu.make_async_copy(hbm_in[n], held[n], in_sem.at[n]) for n in range(18)]
    for n in (4, 3, 5, 6, 7, 16, 10, 11, 2, 1, 0, 8, 9, 17, 12, 13, 14, 15):
        fetches[n].start()

    def need(*ns):
        for n in ns:
            fetches[n].wait()

    def peer_of(k):
        k = jnp.where(k <= 7, k - 1, k)
        n = 7 - lax.rem(k, 8)
        dz = lax.rem(jnp.where(lax.rem(n, 2) == 1, (n + 1) // 2, 8 - n // 2), 8)
        dy = lax.rem(k // 8, 2)
        pr = lax.rem(r // 2 + dz, 8) * 2 + lax.rem(lax.rem(r, 2) + dy, 2)
        return pr, lax.rem(c + k // 16, COLS)

    barrier = pltpu.get_barrier_semaphore()

    def greet(k, _):
        pr, pc = peer_of(k)
        pl.semaphore_signal(barrier, inc=1, device_id=(d, pr, pc), device_id_type=MESH)
        return 0

    lax.fori_loop(1, GROUP, greet, 0)

    lane = lax.broadcasted_iota(jnp.int32, (TJ, CH), 1)
    low = lane < TJ
    row = lax.broadcasted_iota(jnp.int32, (TJ, CH), 0)
    fold = jnp.where(lax.rem(lane, TJ) == row, 1.0, 0.0).astype(BF16)

    def halves(x):
        zero = jnp.zeros_like(x)
        return jnp.concatenate([jnp.where(low, x, zero), jnp.where(low, zero, x)], axis=0)

    def turned(blocks):
        return dot_nt(fold, jnp.concatenate([halves(b) for b in blocks], axis=0).astype(BF16))

    def spread(scratch, s, flat):
        out = turned([flat[h * TJ : (h + 1) * TJ] for h in range(STEP)])
        for h in range(STEP):
            scratch[pl.ds(s * STEP + h, GROUP, stride=TI), :] = out[:, h * CH : (h + 1) * CH]

    def to_peers(count, copy):
        def go(k, _):
            pr, pc = peer_of(k)
            copy(pr, pc)
            return 0

        lax.fori_loop(1, count, go, 0)

    def remote(src, dst, n, pr, pc):
        pltpu.make_async_remote_copy(
            src_ref=src, dst_ref=dst, send_sem=send.at[n], recv_sem=recv.at[n],
            device_id=(d, pr, pc), device_id_type=MESH,
        ).start()

    def scatter(source, target, n):
        to_peers(GROUP, lambda pr, pc: remote(source.at[pr * COLS + pc], target.at[c, r], n, pr, pc))
        target[c, r] = source[mine]

    def scatter_back(source, target, n):
        to_peers(GROUP, lambda pr, pc: remote(source.at[pc, pr], target.at[mine], n, pr, pc))
        target[mine] = source[c, r]

    def wait_for(sem, like, count):
        view = like.at[pl.ds(0, count)]
        pltpu.make_async_copy(view, view, sem).wait()

    def acts(gate, proj, sig, scratch):
        def go(s, _):
            at = pl.ds(s * STEP, STEP)
            sg = sigmoid(gate[at].reshape(SPAN, CH).astype(F32))
            sig[pl.ds(s * SPAN, SPAN), :] = sg
            act = sg * proj[at].reshape(SPAN, CH).astype(F32)
            spread(scratch, s, act.astype(BF16).astype(F32))
            return 0

        lax.fori_loop(0, TURNS, go, 0)

    need(4, 3)
    acts(gate_b, proj_b, sig_b, tmp)
    right_t[...] = tmp[...].astype(BF16).reshape(GROUP, TI, CH)

    need(5, 6, 7, 16, 10, 11)
    g_tri, b_tri = gain_tri[...], bias_tri[...]
    vec_acc[...] = jnp.zeros_like(vec_acc)

    def outer(s, _):
        at, cells = pl.ds(s * STEP, STEP), pl.ds(s * SPAN, SPAN)
        hat, inv = normalize(tri_out[at].reshape(SPAN, CH).astype(F32))
        mixed = (hat * g_tri + b_tri).astype(BF16)
        lifted = dot(mixed, w_out[...])
        sg = sigmoid(gate_out[at].reshape(SPAN, CH).astype(F32))
        up = cotangent[at].reshape(SPAN, CH).astype(F32)
        ups = up * sg
        lift = ups.astype(BF16)
        ggate_s[cells, :] = (ups * lifted * (1.0 - sg)).astype(BF16)
        mixed_s[cells, :] = mixed
        lift_s[cells, :] = lift
        gm = dot_nt(lift, w_out[...])
        vec_acc[0] += fold_rows(gm * hat)
        vec_acc[1] += fold_rows(gm)
        gt = norm_back(gm * g_tri, hat, inv)
        spread(tmp2, s, gt.astype(BF16).astype(F32))
        return 0

    lax.fori_loop(0, TURNS, outer, 0)
    grad_t[...] = tmp2[...].astype(BF16).reshape(GROUP, TI, CH)

    pl.semaphore_wait(barrier, GROUP - 1)
    scatter(right_t, right_r, 0)
    scatter(grad_t, grad_r, 1)

    need(2, 1)
    acts(gate_a, proj_a, sig_a, tmp)
    left_t[...] = tmp[...].astype(BF16).reshape(GROUP, TI, CH)
    scatter(left_t, left_r, 2)

    chunk = r * 2 + c // 2

    def is_summer(odd):
        return lax.rem(r + c + d, 2) == odd

    def to_summers(g, odd):
        def go(k, _):
            n = 7 - lax.rem(k, 8)
            dz = lax.rem(jnp.where(lax.rem(n, 2) == 1, (n + 1) // 2, 8 - n // 2), 8)
            pr = lax.rem(r // 2 + dz, 8) * 2 + lax.rem(lax.rem(r, 2) + lax.rem(k // 8, 2), 2)
            pc = 2 * lax.rem(c // 2 + k // 16, 2) + lax.rem(pr + d + odd, 2)
            there = pr * 2 + pc // 2

            @pl.when(pr * COLS + pc != mine)
            def _():
                remote(part.at[g, there], part_r.at[g, mine], 5 + g, pr, pc)

            return 0

        lax.fori_loop(0, SUMMERS, go, 0)

        @pl.when(is_summer(odd))
        def _():
            part_r[g, mine] = part[g, chunk]

    def sum_up(g, odd):
        @pl.when(is_summer(odd))
        def _():
            wait_for(recv.at[5 + g], part_r.at[g], GROUP - 1)
            final[g, chunk] = jnp.sum(part_r[g], axis=0)
            to_peers(GROUP, lambda pr, pc: remote(final.at[g, chunk], final.at[g, chunk], 8 + g, pr, pc))

    def summed(g, odd):
        @pl.when(is_summer(odd))
        def _():
            wait_for(recv.at[8 + g], final.at[g], SUMMERS - 1)

        @pl.when(jnp.logical_not(is_summer(odd)))
        def _():
            wait_for(recv.at[8 + g], final.at[g], SUMMERS)

    def sums_left(g, odd):
        @pl.when(is_summer(odd))
        def _():
            wait_for(send.at[5 + g], part.at[g], SUMMERS - 1)
            wait_for(send.at[8 + g], part_r.at[g], GROUP - 1)

        @pl.when(jnp.logical_not(is_summer(odd)))
        def _():
            wait_for(send.at[5 + g], part.at[g], SUMMERS)

    odds = (0, 1, 0)
    need(0, 8, 9, 17)
    g_in, b_in = gain_in[...], bias_in[...]

    def first(s, _):
        at, cells = pl.ds(s * STEP, STEP), pl.ds(s * SPAN, SPAN)
        normed, inv = normalize(pair_act[at].reshape(SPAN, CH).astype(F32))
        normed_s[cells, :] = normed
        inv_s[cells, :] = jnp.broadcast_to(inv, (SPAN, CH))
        pn = (normed * g_in + b_in).astype(BF16)
        pn_s[cells, :] = pn
        gn_s[cells, :] = dot_nt(ggate_s[cells, :], w_gate[...])
        return 0

    lax.fori_loop(0, TURNS, first, 0)
    pn_t[...] = pn_s[...].astype(F32).T.astype(BF16)
    part[0, 0:16] = dot_tn(mixed_s[...], lift_s[...]).reshape(16, 8, CH)
    part[0, 16:32] = dot(pn_t[...], ggate_s[...]).reshape(16, 8, CH)
    to_summers(0, odds[0])

    wait_for(recv.at[0], right_t, GROUP - 1)
    for k in range(COLS):
        for j in range(COLS):
            tile = right_r[k, 4 * j : 4 * j + 4].reshape(TJ, CH)
            rbd[j * CH : (j + 1) * CH, k * CH : (k + 1) * CH] = halves(tile.astype(F32)).astype(BF16)
    wait_for(recv.at[1], grad_t, GROUP - 1)
    grads = jnp.concatenate([grad_r[k].reshape(ROWS * TI, CH) for k in range(COLS)], axis=1)
    d_left = dot(grads, rbd[...]).astype(BF16)
    for k in range(COLS):
        dl_s[k] = d_left[:, k * CH : (k + 1) * CH].reshape(ROWS, TI, CH)
    scatter_back(dl_s, dl_r, 3)
    wait_for(recv.at[2], left_t, GROUP - 1)
    lefts = jnp.concatenate([left_r[k].reshape(ROWS * TI, CH) for k in range(COLS)], axis=1)
    d_right = dot_tn(grads, lefts)
    for k in range(COLS):
        for j in range(COLS):
            tile = d_right[j * CH : (j + 1) * CH, k * CH : (k + 1) * CH]
            dr_s[k, 4 * j : 4 * j + 4] = (
                jnp.where(low, tile[:TJ], tile[TJ:]).astype(BF16).reshape(4, TI, CH)
            )
    scatter_back(dr_s, dr_r, 4)
    sum_up(0, odds[0])

    need(12, 13, 14, 15)
    w_a[:, :CH] = w_proj_a[...]
    w_a[:, CH:] = w_gate_a[...]
    w_b[:, :CH] = w_proj_b[...]
    w_b[:, CH:] = w_gate_b[...]

    def side(arr, n, sig, proj, g):
        wait_for(recv.at[n], right_t, GROUP - 1)
        tmp[...] = arr[...].reshape(CELLS, CH).astype(F32)

        def go(s, _):
            at, cells = pl.ds(s * STEP, STEP), pl.ds(s * SPAN, SPAN)
            out = turned([tmp[pl.ds(s * STEP + h, GROUP, stride=TI), :] for h in range(STEP)])
            dd = jnp.concatenate([out[:, h * CH : (h + 1) * CH] for h in range(STEP)], axis=0)
            sg = sig[cells, :]
            ds = dd * sg
            gpg_s[cells, :CH] = ds.astype(BF16)
            gpg_s[cells, CH:] = (ds * proj[at].reshape(SPAN, CH).astype(F32) * (1.0 - sg)).astype(BF16)
            return 0

        lax.fori_loop(0, TURNS, go, 0)
        both = dot(pn_t[...], gpg_s[...])
        part[g, 0:16] = both[:, :CH].reshape(16, 8, CH)
        part[g, 16:32] = both[:, CH:].reshape(16, 8, CH)
        to_summers(g, odds[g])

    side(dl_r, 3, sig_a, proj_a, 1)

    def more(s, _):
        cells = pl.ds(s * SPAN, SPAN)
        gn_s[cells, :] += dot_nt(gpg_s[cells, :], w_a[...])
        return 0

    lax.fori_loop(0, TURNS, more, 0)
    side(dr_r, 4, sig_b, proj_b, 2)

    def last(s, _):
        at, cells = pl.ds(s * STEP, STEP), pl.ds(s * SPAN, SPAN)
        gn = gn_s[cells, :] + dot_nt(gpg_s[cells, :], w_b[...])
        normed = normed_s[cells, :]
        vec_acc[2] += fold_rows(gn * normed)
        vec_acc[3] += fold_rows(gn)
        back = norm_back(gn * g_in, normed, inv_s[cells, :])
        pair_o[at] = back.astype(BF16).reshape(STEP, TJ, CH)
        return 0

    lax.fori_loop(0, TURNS, last, 0)
    for n in range(4):
        vec_s[n : n + 1, :] = jnp.sum(vec_acc[n], axis=0, keepdims=True)
    for k in range(1, COLS):
        remote(vec_s, vec_r.at[c], 11, r, lax.rem(c + k, COLS))
    vec_r[c] = vec_s[...]
    sum_up(1, odds[1])
    wait_for(recv.at[11], vec_r, COLS - 1)
    vec_c[...] = jnp.sum(vec_r[...], axis=0)

    def over_rows(k, _):
        remote(vec_c, vec_a.at[r], 12, lax.rem(r + k, ROWS), c)
        return 0

    lax.fori_loop(1, ROWS, over_rows, 0)
    vec_a[r] = vec_c[...]
    sum_up(2, odds[2])

    wait_for(recv.at[12], vec_a, ROWS - 1)
    vec_o[...] = jnp.sum(vec_a[...], axis=0)
    for g, outs in ((1, (0, 1)), (0, (4, 5)), (2, (2, 3))):
        summed(g, odds[g])
        w_o[outs[0]][...] = final[g, 0:16]
        w_o[outs[1]][...] = final[g, 16:32]
    for n in range(5):
        wait_for(send.at[n], right_t, GROUP - 1)
    for g in range(3):
        sums_left(g, odds[g])
    wait_for(send.at[11], vec_r, COLS - 1)
    wait_for(send.at[12], vec_a, ROWS - 1)


def hand_out(*refs):
    (pair_in, vec_in, *w_in), (pair_o, *vec_o), w_o, sem = refs[:8], refs[8:13], refs[13:19], refs[19]
    copies = [pltpu.make_async_copy(pair_in, pair_o, sem.at[0])]
    for n in range(4):
        copies.append(pltpu.make_async_copy(vec_in.at[pl.ds(n, 1)], vec_o[n], sem.at[1 + n]))
    for n in range(6):
        copies.append(pltpu.make_async_copy(w_in[n], w_o[n], sem.at[5 + n]))
    for copy in copies:
        copy.start()
    for copy in copies:
        copy.wait()


def local(
    pair_act, gain_in, bias_in, proj_a, gate_a, proj_b, gate_b, tri_out, gain_tri, bias_tri,
    gate_out, cotangent, w_proj_a, w_gate_a, w_proj_b, w_gate_b, w_out, w_gate,
):
    args = (
        pair_act, proj_a, gate_a, proj_b, gate_b, tri_out, gate_out, cotangent,
        gain_in.reshape(1, CH), bias_in.reshape(1, CH), gain_tri.reshape(1, CH), bias_tri.reshape(1, CH),
        w_proj_a, w_gate_a, w_proj_b, w_gate_b, w_out, w_gate,
    )
    hbm = pl.BlockSpec(memory_space=pltpu.HBM)
    vmem = pl.BlockSpec(memory_space=pltpu.VMEM)
    square = jax.ShapeDtypeStruct((16, 8, CH), F32)
    turned = pltpu.VMEM((GROUP, TI, CH), BF16)
    landed = pltpu.VMEM((COLS, ROWS, TI, CH), BF16)
    wide = pltpu.VMEM((CELLS, CH), F32)
    half = pltpu.VMEM((CELLS, CH), BF16)
    outs = pl.pallas_call(
        kernel,
        out_shape=(
            jax.ShapeDtypeStruct(pair_act.shape, BF16),
            jax.ShapeDtypeStruct((4, CH), F32),
            square, square, square, square, square, square,
        ),
        in_specs=[hbm] * 18,
        out_specs=tuple([vmem] * 8),
        scratch_shapes=[pltpu.VMEM(a.shape, a.dtype) for a in args] + [
            wide, wide, turned, turned, turned, landed, landed, landed,
            landed, landed, turned, turned, pltpu.VMEM((4 * CH, 4 * CH), BF16),
            wide, wide, half, half, half, wide, wide, half, pltpu.VMEM((CH, CELLS), BF16), wide,
            pltpu.VMEM((CELLS, 2 * CH), BF16), pltpu.VMEM((CH, 2 * CH), BF16), pltpu.VMEM((CH, 2 * CH), BF16),
            pltpu.VMEM((3, SUMMERS, 8, CH), F32), pltpu.VMEM((3, GROUP, 8, CH), F32),
            pltpu.VMEM((3, SUMMERS, 8, CH), F32), pltpu.VMEM((4, 8, CH), F32),
            pltpu.VMEM((4, CH), F32), pltpu.VMEM((COLS, 4, CH), F32),
            pltpu.VMEM((4, CH), F32), pltpu.VMEM((ROWS, 4, CH), F32),
            pltpu.SemaphoreType.DMA((18,)),
            pltpu.SemaphoreType.DMA((13,)), pltpu.SemaphoreType.DMA((13,)),
        ],
        compiler_params=pltpu.CompilerParams(
            collective_id=0, has_side_effects=True, vmem_limit_bytes=63 * 1024 * 1024
        ),
        name="triangle_backward",
    )(*args)
    vector = jax.ShapeDtypeStruct((1, CH), F32)
    pair_grad, v0, v1, v2, v3, *weights = pl.pallas_call(
        hand_out,
        out_shape=(jax.ShapeDtypeStruct(pair_act.shape, BF16),) + (vector,) * 4 + (square,) * 6,
        in_specs=[vmem] * 8,
        out_specs=tuple([hbm] * 11),
        scratch_shapes=[pltpu.SemaphoreType.DMA((11,))],
        name="hand_out",
    )(*outs)
    vecs = [v.reshape(CH) for v in (v2, v3, v0, v1)]
    return (pair_grad, *vecs, *[w.reshape(CH, CH) for w in weights])


def solution(mesh):
    tile = P(("dp", "row"), "col", None)
    placed = (
        tile, P(), P(), tile, tile, tile, tile, tile, P(), P(),
        tile, tile, P(), P(), P(), P(), P(), P(),
    )
    vector, matrix = P("dp"), P("dp", None)
    return jax.shard_map(
        local,
        mesh=mesh,
        in_specs=placed,
        out_specs=(tile,) + (vector,) * 4 + (matrix,) * 6,
        check_vma=False,
    )
```

```python
import jax
import jax.numpy as jnp
from jax import lax
from jax.experimental import pallas as pl
from jax.experimental.pallas import tpu as pltpu
from jax.sharding import PartitionSpec as P

MESH = pl.DeviceIdType.MESH
F32 = jnp.float32
BF16 = jnp.bfloat16
ROWS = 16
COLS = 4
GROUP = ROWS * COLS
TI = 16
TJ = 64
CELLS = TI * TJ
CH = 128
STEP = 2
TURNS = TI // STEP
SPAN = STEP * TJ
BIG = 8


def dot(a, b):
    return jnp.dot(a, b, preferred_element_type=F32)


def dot_nt(a, b):
    return lax.dot_general(a, b, (((1,), (1,)), ((), ())), preferred_element_type=F32)


def dot_tn(a, b):
    return lax.dot_general(a, b, (((0,), (0,)), ((), ())), preferred_element_type=F32)


def sigmoid(x):
    return 1.0 / (1.0 + jnp.exp(-x))


def normalize(values):
    average = jnp.mean(values, axis=-1, keepdims=True)
    centred = values - average
    inverse = lax.rsqrt(jnp.mean(centred * centred, axis=-1, keepdims=True) + 1e-05)
    return centred * inverse, inverse


def norm_back(grad_hat, normed, inverse):
    grad_mean = jnp.mean(grad_hat, axis=-1, keepdims=True)
    grad_corr = jnp.mean(grad_hat * normed, axis=-1, keepdims=True)
    return inverse * (grad_hat - grad_mean - normed * grad_corr)


def fold_rows(x):
    return jnp.sum(x.reshape(-1, 8, CH), axis=0)


def kernel(*refs):
    hbm_in, refs = refs[:18], refs[18:]
    (pair_o, vec_o, *w_o), refs = refs[:8], refs[8:]
    held, refs = refs[:18], refs[18:]
    (pair_act, proj_a, gate_a, proj_b, gate_b, tri_out, gate_out, cotangent,
     gain_in, bias_in, gain_tri, bias_tri,
     w_proj_a, w_gate_a, w_proj_b, w_gate_b, w_out, w_gate) = held
    (tmp, tmp2, left_t, right_t, grad_t, left_r, right_r, grad_r,
     dl_s, dr_s, dl_r, dr_r, rbd,
     sig_a, sig_b, mixed_s, lift_s, ggate_s, normed_s, inv_s, pn_s, pn_t, gn_s, gpg_s, w_a, w_b,
     part, part_r, final, vec_acc, vec_s, vec_r, vec_c, vec_a,
     in_sem, send, recv) = refs
    d, r, c = lax.axis_index("dp"), lax.axis_index("row"), lax.axis_index("col")
    mine = r * COLS + c

    fetches = [pltpu.make_async_copy(hbm_in[n], held[n], in_sem.at[n]) for n in range(18)]
    for n in (4, 3, 5, 6, 7, 16, 10, 11, 2, 1, 0, 8, 9, 17, 12, 13, 14, 15):
        fetches[n].start()

    def need(*ns):
        for n in ns:
            fetches[n].wait()

    def peer_of(k):
        k = GROUP - k
        n = lax.rem(k, 8)
        dz = lax.rem(jnp.where(lax.rem(n, 2) == 1, (n + 1) // 2, 8 - n // 2), 8)
        dy = lax.rem(k // 8, 2)
        pr = lax.rem(r // 2 + dz, 8) * 2 + lax.rem(lax.rem(r, 2) + dy, 2)
        return pr, lax.rem(c + k // 16, COLS)

    barrier = pltpu.get_barrier_semaphore()

    def greet(k, _):
        pr, pc = peer_of(k)
        pl.semaphore_signal(barrier, inc=1, device_id=(d, pr, pc), device_id_type=MESH)
        return 0

    lax.fori_loop(1, GROUP, greet, 0)

    lane = lax.broadcasted_iota(jnp.int32, (TJ, CH), 1)
    low = lane < TJ
    row = lax.broadcasted_iota(jnp.int32, (TJ, CH), 0)
    fold = jnp.where(lax.rem(lane, TJ) == row, 1.0, 0.0).astype(BF16)

    def halves(x):
        zero = jnp.zeros_like(x)
        return jnp.concatenate([jnp.where(low, x, zero), jnp.where(low, zero, x)], axis=0)

    def turned(blocks):
        return dot_nt(fold, jnp.concatenate([halves(b) for b in blocks], axis=0).astype(BF16))

    def spread(scratch, s, flat):
        out = turned([flat[h * TJ : (h + 1) * TJ] for h in range(STEP)])
        for h in range(STEP):
            scratch[pl.ds(s * STEP + h, GROUP, stride=TI), :] = out[:, h * CH : (h + 1) * CH]

    def to_peers(count, copy):
        def go(k, _):
            pr, pc = peer_of(k)
            copy(pr, pc)
            return 0

        lax.fori_loop(1, count, go, 0)

    def remote(src, dst, n, pr, pc):
        pltpu.make_async_remote_copy(
            src_ref=src, dst_ref=dst, send_sem=send.at[n], recv_sem=recv.at[n],
            device_id=(d, pr, pc), device_id_type=MESH,
        ).start()

    def scatter(source, target, n):
        to_peers(GROUP, lambda pr, pc: remote(source.at[pr * COLS + pc], target.at[c, r], n, pr, pc))
        target[c, r] = source[mine]

    def scatter_back(source, target, n):
        to_peers(GROUP, lambda pr, pc: remote(source.at[pc, pr], target.at[mine], n, pr, pc))
        target[mine] = source[c, r]

    def wait_for(sem, like, count):
        view = like.at[pl.ds(0, count)]
        pltpu.make_async_copy(view, view, sem).wait()

    def acts(gate, proj, sig, scratch):
        def go(s, _):
            at = pl.ds(s * STEP, STEP)
            sg = sigmoid(gate[at].reshape(SPAN, CH).astype(F32))
            sig[pl.ds(s * SPAN, SPAN), :] = sg
            act = sg * proj[at].reshape(SPAN, CH).astype(F32)
            spread(scratch, s, act.astype(BF16).astype(F32))
            return 0

        lax.fori_loop(0, TURNS, go, 0, unroll=TURNS)

    need(4, 3)
    acts(gate_b, proj_b, sig_b, tmp)
    right_t[...] = tmp[...].astype(BF16).reshape(GROUP, TI, CH)

    pl.semaphore_wait(barrier, GROUP - 1)
    scatter(right_t, right_r, 0)

    need(5, 6, 7, 16, 10, 11)
    g_tri, b_tri = gain_tri[...], bias_tri[...]
    vec_acc[...] = jnp.zeros_like(vec_acc)

    def outer(s, _):
        at, cells = pl.ds(s * STEP, STEP), pl.ds(s * SPAN, SPAN)
        hat, inv = normalize(tri_out[at].reshape(SPAN, CH).astype(F32))
        mixed = (hat * g_tri + b_tri).astype(BF16)
        lifted = dot(mixed, w_out[...])
        sg = sigmoid(gate_out[at].reshape(SPAN, CH).astype(F32))
        up = cotangent[at].reshape(SPAN, CH).astype(F32)
        ups = up * sg
        lift = ups.astype(BF16)
        ggate_s[cells, :] = (ups * lifted * (1.0 - sg)).astype(BF16)
        mixed_s[cells, :] = mixed
        lift_s[cells, :] = lift
        gm = dot_nt(lift, w_out[...])
        vec_acc[0] += fold_rows(gm * hat)
        vec_acc[1] += fold_rows(gm)
        gt = norm_back(gm * g_tri, hat, inv)
        spread(tmp2, s, gt.astype(BF16).astype(F32))
        return 0

    lax.fori_loop(0, TURNS, outer, 0, unroll=TURNS)
    grad_t[...] = tmp2[...].astype(BF16).reshape(GROUP, TI, CH)

    scatter(grad_t, grad_r, 1)

    need(2, 1)
    acts(gate_a, proj_a, sig_a, tmp)
    left_t[...] = tmp[...].astype(BF16).reshape(GROUP, TI, CH)
    scatter(left_t, left_r, 2)

    def summer_col(g, on_row):
        return lax.rem(on_row + on_row // 4 + g + d, COLS)

    def is_summer(g):
        return c == summer_col(g, r)

    def to_summers(g):
        def go(k, _):
            n = 7 - lax.rem(k, 8)
            dz = lax.rem(jnp.where(lax.rem(n, 2) == 1, (n + 1) // 2, 8 - n // 2), 8)
            pr = lax.rem(r // 2 + dz, 8) * 2 + lax.rem(lax.rem(r, 2) + k // 8, 2)
            pc = summer_col(g, pr)

            @pl.when(pr * COLS + pc != mine)
            def _():
                remote(part.at[g, pr], part_r.at[g, mine], 5 + g, pr, pc)

            return 0

        lax.fori_loop(0, ROWS, go, 0)

        @pl.when(is_summer(g))
        def _():
            part_r[g, mine] = part[g, r]

    def sum_up(g):
        @pl.when(is_summer(g))
        def _():
            wait_for(recv.at[5 + g], part_r.at[g], GROUP - 1)
            final[g, r] = jnp.sum(part_r[g].astype(F32), axis=0).astype(final.dtype)
            to_peers(GROUP, lambda pr, pc: remote(final.at[g, r], final.at[g, r], 8 + g, pr, pc))

    def summed(g):
        @pl.when(is_summer(g))
        def _():
            wait_for(recv.at[8 + g], final.at[g], ROWS - 1)

        @pl.when(jnp.logical_not(is_summer(g)))
        def _():
            wait_for(recv.at[8 + g], final.at[g], ROWS)

    def sums_left(g):
        @pl.when(is_summer(g))
        def _():
            wait_for(send.at[5 + g], part.at[g], ROWS - 1)
            wait_for(send.at[8 + g], part_r.at[g], GROUP - 1)

        @pl.when(jnp.logical_not(is_summer(g)))
        def _():
            wait_for(send.at[5 + g], part.at[g], ROWS)

    need(0, 8, 9, 17)
    g_in, b_in = gain_in[...], bias_in[...]

    def first(s, _):
        at, cells = pl.ds(s * STEP, STEP), pl.ds(s * SPAN, SPAN)
        normed, inv = normalize(pair_act[at].reshape(SPAN, CH).astype(F32))
        normed_s[cells, :] = normed
        inv_s[cells, :] = jnp.broadcast_to(inv, (SPAN, CH))
        pn = (normed * g_in + b_in).astype(BF16)
        pn_s[cells, :] = pn
        gn_s[cells, :] = dot_nt(ggate_s[cells, :], w_gate[...])
        return 0

    lax.fori_loop(0, TURNS, first, 0, unroll=TURNS)
    pn_t[...] = pn_s[...].astype(F32).T.astype(BF16)
    part[0, 0:8] = dot_tn(mixed_s[...], lift_s[...]).astype(BF16).reshape(8, 16, CH)
    part[0, 8:16] = dot(pn_t[...], ggate_s[...]).astype(BF16).reshape(8, 16, CH)
    to_summers(0)

    wait_for(recv.at[0], right_t, GROUP - 1)
    for k in range(COLS):
        for j in range(COLS):
            tile = right_r[k, 4 * j : 4 * j + 4].reshape(TJ, CH)
            rbd[j * CH : (j + 1) * CH, k * CH : (k + 1) * CH] = halves(tile.astype(F32)).astype(BF16)
    wait_for(recv.at[1], grad_t, GROUP - 1)
    grads = jnp.concatenate([grad_r[k].reshape(ROWS * TI, CH) for k in range(COLS)], axis=1)
    d_left = dot(grads, rbd[...]).astype(BF16)
    for k in range(COLS):
        dl_s[k] = d_left[:, k * CH : (k + 1) * CH].reshape(ROWS, TI, CH)
    scatter_back(dl_s, dl_r, 3)
    wait_for(recv.at[2], left_t, GROUP - 1)
    lefts = jnp.concatenate([left_r[k].reshape(ROWS * TI, CH) for k in range(COLS)], axis=1)
    d_right = dot_tn(grads, lefts)
    for k in range(COLS):
        for j in range(COLS):
            tile = d_right[j * CH : (j + 1) * CH, k * CH : (k + 1) * CH]
            dr_s[k, 4 * j : 4 * j + 4] = (
                jnp.where(low, tile[:TJ], tile[TJ:]).astype(BF16).reshape(4, TI, CH)
            )
    scatter_back(dr_s, dr_r, 4)
    sum_up(0)

    need(12, 13, 14, 15)
    w_a[:, :CH] = w_proj_a[...]
    w_a[:, CH:] = w_gate_a[...]
    w_b[:, :CH] = w_proj_b[...]
    w_b[:, CH:] = w_gate_b[...]

    def side(arr, n, sig, proj, g):
        wait_for(recv.at[n], right_t, GROUP - 1)
        tmp[...] = arr[...].reshape(CELLS, CH).astype(F32)

        def go(s, _):
            at, cells = pl.ds(s * STEP, STEP), pl.ds(s * SPAN, SPAN)
            out = turned([tmp[pl.ds(s * STEP + h, GROUP, stride=TI), :] for h in range(STEP)])
            dd = jnp.concatenate([out[:, h * CH : (h + 1) * CH] for h in range(STEP)], axis=0)
            sg = sig[cells, :]
            ds = dd * sg
            gpg_s[cells, :CH] = ds.astype(BF16)
            gpg_s[cells, CH:] = (ds * proj[at].reshape(SPAN, CH).astype(F32) * (1.0 - sg)).astype(BF16)
            return 0

        lax.fori_loop(0, TURNS, go, 0, unroll=TURNS)
        both = dot(pn_t[...], gpg_s[...])
        part[g, 0:8] = both[:, :CH].astype(BF16).reshape(8, 16, CH)
        part[g, 8:16] = both[:, CH:].astype(BF16).reshape(8, 16, CH)
        to_summers(g)

    side(dl_r, 3, sig_a, proj_a, 1)

    def more(s, _):
        cells = pl.ds(s * SPAN, SPAN)
        gn_s[cells, :] += dot_nt(gpg_s[cells, :], w_a[...])
        return 0

    lax.fori_loop(0, TURNS, more, 0, unroll=TURNS)
    side(dr_r, 4, sig_b, proj_b, 2)

    def last(s, _):
        at, cells = pl.ds(s * STEP, STEP), pl.ds(s * SPAN, SPAN)
        gn = gn_s[cells, :] + dot_nt(gpg_s[cells, :], w_b[...])
        normed = normed_s[cells, :]
        vec_acc[2] += fold_rows(gn * normed)
        vec_acc[3] += fold_rows(gn)
        back = norm_back(gn * g_in, normed, inv_s[cells, :])
        pair_o[at] = back.astype(BF16).reshape(STEP, TJ, CH)
        return 0

    lax.fori_loop(0, TURNS, last, 0, unroll=TURNS)
    for n in range(4):
        vec_s[n : n + 1, :] = jnp.sum(vec_acc[n], axis=0, keepdims=True)
    for k in range(1, COLS):
        remote(vec_s, vec_r.at[c], 11, r, lax.rem(c + k, COLS))
    vec_r[c] = vec_s[...]
    sum_up(1)
    wait_for(recv.at[11], vec_r, COLS - 1)
    vec_c[...] = jnp.sum(vec_r[...], axis=0)

    def over_rows(k, _):
        remote(vec_c, vec_a.at[r], 12, lax.rem(r + k, ROWS), c)
        return 0

    lax.fori_loop(1, ROWS, over_rows, 0)
    vec_a[r] = vec_c[...]
    sum_up(2)

    wait_for(recv.at[12], vec_a, ROWS - 1)
    vec_o[...] = jnp.sum(vec_a[...], axis=0)
    for g, outs in ((1, (0, 1)), (0, (4, 5)), (2, (2, 3))):
        summed(g)
        w_o[outs[0]][...] = final[g, 0:8].astype(F32).reshape(CH, CH)
        w_o[outs[1]][...] = final[g, 8:16].astype(F32).reshape(CH, CH)
    for n in range(5):
        wait_for(send.at[n], right_t, GROUP - 1)
    for g in range(3):
        sums_left(g)
    wait_for(send.at[11], vec_r, COLS - 1)
    wait_for(send.at[12], vec_a, ROWS - 1)


def hand_out(*refs):
    (pair_in, vec_in, *w_in), (pair_o, *vec_o), w_o, sem = refs[:8], refs[8:13], refs[13:19], refs[19]
    copies = [pltpu.make_async_copy(pair_in, pair_o, sem.at[0])]
    for n in range(4):
        copies.append(pltpu.make_async_copy(vec_in.at[pl.ds(n, 1)], vec_o[n], sem.at[1 + n]))
    for n in range(6):
        copies.append(pltpu.make_async_copy(w_in[n], w_o[n], sem.at[5 + n]))
    for copy in copies:
        copy.start()
    for copy in copies:
        copy.wait()


def local(
    pair_act, gain_in, bias_in, proj_a, gate_a, proj_b, gate_b, tri_out, gain_tri, bias_tri,
    gate_out, cotangent, w_proj_a, w_gate_a, w_proj_b, w_gate_b, w_out, w_gate,
):
    args = (
        pair_act, proj_a, gate_a, proj_b, gate_b, tri_out, gate_out, cotangent,
        gain_in.reshape(1, CH), bias_in.reshape(1, CH), gain_tri.reshape(1, CH), bias_tri.reshape(1, CH),
        w_proj_a, w_gate_a, w_proj_b, w_gate_b, w_out, w_gate,
    )
    hbm = pl.BlockSpec(memory_space=pltpu.HBM)
    vmem = pl.BlockSpec(memory_space=pltpu.VMEM)
    square = jax.ShapeDtypeStruct((CH, CH), F32)
    turned = pltpu.VMEM((GROUP, TI, CH), BF16)
    landed = pltpu.VMEM((COLS, ROWS, TI, CH), BF16)
    wide = pltpu.VMEM((CELLS, CH), F32)
    half = pltpu.VMEM((CELLS, CH), BF16)
    outs = pl.pallas_call(
        kernel,
        out_shape=(
            jax.ShapeDtypeStruct(pair_act.shape, BF16),
            jax.ShapeDtypeStruct((4, CH), F32),
            square, square, square, square, square, square,
        ),
        in_specs=[hbm] * 18,
        out_specs=tuple([vmem] * 8),
        scratch_shapes=[pltpu.VMEM(a.shape, a.dtype) for a in args] + [
            wide, wide, turned, turned, turned, landed, landed, landed,
            landed, landed, turned, turned, pltpu.VMEM((4 * CH, 4 * CH), BF16),
            wide, wide, half, half, half, wide, wide, half, pltpu.VMEM((CH, CELLS), BF16), wide,
            pltpu.VMEM((CELLS, 2 * CH), BF16), pltpu.VMEM((CH, 2 * CH), BF16), pltpu.VMEM((CH, 2 * CH), BF16),
            pltpu.VMEM((3, ROWS, 16, CH), BF16), pltpu.VMEM((3, GROUP, 16, CH), BF16),
            pltpu.VMEM((3, ROWS, 16, CH), BF16), pltpu.VMEM((4, 8, CH), F32),
            pltpu.VMEM((4, CH), F32), pltpu.VMEM((COLS, 4, CH), F32),
            pltpu.VMEM((4, CH), F32), pltpu.VMEM((ROWS, 4, CH), F32),
            pltpu.SemaphoreType.DMA((18,)),
            pltpu.SemaphoreType.DMA((13,)), pltpu.SemaphoreType.DMA((13,)),
        ],
        compiler_params=pltpu.CompilerParams(
            collective_id=0, has_side_effects=True, vmem_limit_bytes=63 * 1024 * 1024
        ),
        name="triangle_backward",
    )(*args)
    vector = jax.ShapeDtypeStruct((1, CH), F32)
    pair_grad, v0, v1, v2, v3, *weights = pl.pallas_call(
        hand_out,
        out_shape=(jax.ShapeDtypeStruct(pair_act.shape, BF16),) + (vector,) * 4 + (square,) * 6,
        in_specs=[vmem] * 8,
        out_specs=tuple([hbm] * 11),
        scratch_shapes=[pltpu.SemaphoreType.DMA((11,))],
        name="hand_out",
    )(*outs)
    vecs = [v.reshape(CH) for v in (v2, v3, v0, v1)]
    return (pair_grad, *vecs, *weights)


def solution(mesh):
    tile = P(("dp", "row"), "col", None)
    placed = (
        tile, P(), P(), tile, tile, tile, tile, tile, P(), P(),
        tile, tile, P(), P(), P(), P(), P(), P(),
    )
    vector, matrix = P("dp"), P("dp", None)
    return jax.shard_map(
        local,
        mesh=mesh,
        in_specs=placed,
        out_specs=(tile,) + (vector,) * 4 + (matrix,) * 6,
        check_vma=False,
    )
```

```python
import jax
import jax.numpy as jnp
from jax import lax
from jax.experimental import pallas as pl
from jax.experimental.pallas import tpu as pltpu
from jax.sharding import PartitionSpec as P

MESH = pl.DeviceIdType.MESH
F32 = jnp.float32
BF16 = jnp.bfloat16
ROWS = 16
COLS = 4
GROUP = ROWS * COLS
TI = 16
TJ = 64
CELLS = TI * TJ
CH = 128
STEP = 2
TURNS = TI // STEP
SPAN = STEP * TJ
BIG = 8


def dot(a, b):
    return jnp.dot(a, b, preferred_element_type=F32)


def dot_nt(a, b):
    return lax.dot_general(a, b, (((1,), (1,)), ((), ())), preferred_element_type=F32)


def dot_tn(a, b):
    return lax.dot_general(a, b, (((0,), (0,)), ((), ())), preferred_element_type=F32)


def sigmoid(x):
    return 1.0 / (1.0 + jnp.exp(-x))


def normalize(values):
    average = jnp.mean(values, axis=-1, keepdims=True)
    centred = values - average
    inverse = lax.rsqrt(jnp.mean(centred * centred, axis=-1, keepdims=True) + 1e-05)
    return centred * inverse, inverse


def norm_back(grad_hat, normed, inverse):
    grad_mean = jnp.mean(grad_hat, axis=-1, keepdims=True)
    grad_corr = jnp.mean(grad_hat * normed, axis=-1, keepdims=True)
    return inverse * (grad_hat - grad_mean - normed * grad_corr)


def alternate(n):
    return lax.rem(jnp.where(lax.rem(n, 2) == 1, (n + 1) // 2, 8 - n // 2), 8)


def fold_rows(x):
    return jnp.sum(x.reshape(-1, 8, CH), axis=0)


def kernel(*refs):
    hbm_in, refs = refs[:18], refs[18:]
    (pair_o, vec_o, *w_o), refs = refs[:8], refs[8:]
    held, refs = refs[:18], refs[18:]
    (pair_act, proj_a, gate_a, proj_b, gate_b, tri_out, gate_out, cotangent,
     gain_in, bias_in, gain_tri, bias_tri,
     w_proj_a, w_gate_a, w_proj_b, w_gate_b, w_out, w_gate) = held
    (tmp, tmp2, left_t, right_t, grad_t, left_r, right_r, grad_r,
     dl_s, dr_s, dl_r, dr_r, rbd,
     sig_a, sig_b, mixed_s, lift_s, ggate_s, normed_s, inv_s, pn_s, pn_t, gn_s, gpg_s, w_a, w_b,
     part, part_r, final, tail_p, tail_z, tail_s, tail_x, tail_t, tail_f,
     vec_acc, vec_s, vec_r, vec_c, vec_a,
     in_sem, send, recv) = refs
    d, r, c = lax.axis_index("dp"), lax.axis_index("row"), lax.axis_index("col")
    mine = r * COLS + c

    fetches = [pltpu.make_async_copy(hbm_in[n], held[n], in_sem.at[n]) for n in range(18)]
    for n in (4, 3, 5, 6, 7, 16, 10, 11, 2, 1, 0, 8, 9, 17, 12, 13, 14, 15):
        fetches[n].start()

    def need(*ns):
        for n in ns:
            fetches[n].wait()

    cols = [lax.rem(c + k, COLS) for k in range(COLS)]

    def to_peers(copy):
        def go(k, _):
            k = ROWS - k
            pr = lax.rem(r // 2 + alternate(lax.rem(k, 8)), 8) * 2 + lax.rem(lax.rem(r, 2) + k // 8, 2)
            for n in (2, 1, 3, 0):
                copy(pr, cols[n])
            return 0

        lax.fori_loop(1, ROWS, go, 0)
        for n in (2, 1, 3):
            copy(r, cols[n])

    barrier = pltpu.get_barrier_semaphore()

    def greet(pr, pc):
        pl.semaphore_signal(barrier, inc=1, device_id=(d, pr, pc), device_id_type=MESH)

    to_peers(greet)

    lane = lax.broadcasted_iota(jnp.int32, (TJ, CH), 1)
    low = lane < TJ
    row = lax.broadcasted_iota(jnp.int32, (TJ, CH), 0)
    fold = jnp.where(lax.rem(lane, TJ) == row, 1.0, 0.0).astype(BF16)

    def halves(x):
        zero = jnp.zeros_like(x)
        return jnp.concatenate([jnp.where(low, x, zero), jnp.where(low, zero, x)], axis=0)

    def turned(blocks):
        return dot_nt(fold, jnp.concatenate([halves(b) for b in blocks], axis=0).astype(BF16))

    def spread(scratch, s, flat):
        out = turned([flat[h * TJ : (h + 1) * TJ] for h in range(STEP)])
        for h in range(STEP):
            scratch[pl.ds(s * STEP + h, GROUP, stride=TI), :] = out[:, h * CH : (h + 1) * CH]

    def remote(src, dst, n, pr, pc):
        pltpu.make_async_remote_copy(
            src_ref=src, dst_ref=dst, send_sem=send.at[n], recv_sem=recv.at[n],
            device_id=(d, pr, pc), device_id_type=MESH,
        ).start()

    def scatter(source, target, n):
        to_peers(lambda pr, pc: remote(source.at[pr * COLS + pc], target.at[c, r], n, pr, pc))
        target[c, r] = source[mine]

    def scatter_back(source, target, n):
        to_peers(lambda pr, pc: remote(source.at[pc, pr], target.at[mine], n, pr, pc))
        target[mine] = source[c, r]

    def wait_for(sem, like, count):
        view = like.at[pl.ds(0, count)]
        pltpu.make_async_copy(view, view, sem).wait()

    def acts(gate, proj, sig, scratch):
        def go(s, _):
            at = pl.ds(s * STEP, STEP)
            sg = sigmoid(gate[at].reshape(SPAN, CH).astype(F32))
            sig[pl.ds(s * SPAN, SPAN), :] = sg
            act = sg * proj[at].reshape(SPAN, CH).astype(F32)
            spread(scratch, s, act.astype(BF16).astype(F32))
            return 0

        lax.fori_loop(0, TURNS, go, 0, unroll=TURNS)

    need(4, 3)
    acts(gate_b, proj_b, sig_b, tmp)
    right_t[...] = tmp[...].astype(BF16).reshape(GROUP, TI, CH)

    pl.semaphore_wait(barrier, GROUP - 1)
    scatter(right_t, right_r, 0)

    need(5, 6, 7, 16, 10, 11)
    g_tri, b_tri = gain_tri[...], bias_tri[...]
    vec_acc[...] = jnp.zeros_like(vec_acc)

    def outer(s, _):
        at, cells = pl.ds(s * STEP, STEP), pl.ds(s * SPAN, SPAN)
        hat, inv = normalize(tri_out[at].reshape(SPAN, CH).astype(F32))
        mixed = (hat * g_tri + b_tri).astype(BF16)
        lifted = dot(mixed, w_out[...])
        sg = sigmoid(gate_out[at].reshape(SPAN, CH).astype(F32))
        up = cotangent[at].reshape(SPAN, CH).astype(F32)
        ups = up * sg
        lift = ups.astype(BF16)
        ggate_s[cells, :] = (ups * lifted * (1.0 - sg)).astype(BF16)
        mixed_s[cells, :] = mixed
        lift_s[cells, :] = lift
        gm = dot_nt(lift, w_out[...])
        vec_acc[0] += fold_rows(gm * hat)
        vec_acc[1] += fold_rows(gm)
        gt = norm_back(gm * g_tri, hat, inv)
        spread(tmp2, s, gt.astype(BF16).astype(F32))
        return 0

    lax.fori_loop(0, TURNS, outer, 0, unroll=TURNS)
    grad_t[...] = tmp2[...].astype(BF16).reshape(GROUP, TI, CH)

    scatter(grad_t, grad_r, 1)

    need(2, 1)
    acts(gate_a, proj_a, sig_a, tmp)
    left_t[...] = tmp[...].astype(BF16).reshape(GROUP, TI, CH)
    scatter(left_t, left_r, 2)

    def summer_col(g, on_row):
        return lax.rem(on_row + on_row // 4 + g + d, COLS)

    def is_summer(g):
        return c == summer_col(g, r)

    def to_summers(g):
        def go(k, _):
            n = 7 - lax.rem(k, 8)
            dz = alternate(n)
            pr = lax.rem(r // 2 + dz, 8) * 2 + lax.rem(lax.rem(r, 2) + k // 8, 2)
            pc = summer_col(g, pr)

            @pl.when(pr * COLS + pc != mine)
            def _():
                remote(part.at[g, pr], part_r.at[g, mine], 5 + g, pr, pc)

            return 0

        lax.fori_loop(0, ROWS, go, 0)

        @pl.when(is_summer(g))
        def _():
            part_r[g, mine] = part[g, r]

    def sum_up(g):
        @pl.when(is_summer(g))
        def _():
            wait_for(recv.at[5 + g], part_r.at[g], GROUP - 1)
            final[g, r] = jnp.sum(part_r[g].astype(F32), axis=0).astype(final.dtype)
            to_peers(lambda pr, pc: remote(final.at[g, r], final.at[g, r], 8 + g, pr, pc))

    def summed(g):
        @pl.when(is_summer(g))
        def _():
            wait_for(recv.at[8 + g], final.at[g], ROWS - 1)

        @pl.when(jnp.logical_not(is_summer(g)))
        def _():
            wait_for(recv.at[8 + g], final.at[g], ROWS)

    def sums_left(g):
        @pl.when(is_summer(g))
        def _():
            wait_for(send.at[5 + g], part.at[g], ROWS - 1)
            wait_for(send.at[8 + g], part_r.at[g], GROUP - 1)

        @pl.when(jnp.logical_not(is_summer(g)))
        def _():
            wait_for(send.at[5 + g], part.at[g], ROWS)

    need(0, 8, 9, 17)
    g_in, b_in = gain_in[...], bias_in[...]

    def first(s, _):
        at, cells = pl.ds(s * STEP, STEP), pl.ds(s * SPAN, SPAN)
        normed, inv = normalize(pair_act[at].reshape(SPAN, CH).astype(F32))
        normed_s[cells, :] = normed
        inv_s[cells, :] = jnp.broadcast_to(inv, (SPAN, CH))
        pn = (normed * g_in + b_in).astype(BF16)
        pn_s[cells, :] = pn
        gn_s[cells, :] = dot_nt(ggate_s[cells, :], w_gate[...])
        return 0

    lax.fori_loop(0, TURNS, first, 0, unroll=TURNS)
    pn_t[...] = pn_s[...].astype(F32).T.astype(BF16)
    part[0, 0:8] = dot_tn(mixed_s[...], lift_s[...]).astype(BF16).reshape(8, 16, CH)
    part[0, 8:16] = dot(pn_t[...], ggate_s[...]).astype(BF16).reshape(8, 16, CH)
    to_summers(0)

    wait_for(recv.at[0], right_t, GROUP - 1)
    for k in range(COLS):
        for j in range(COLS):
            tile = right_r[k, 4 * j : 4 * j + 4].reshape(TJ, CH)
            rbd[j * CH : (j + 1) * CH, k * CH : (k + 1) * CH] = halves(tile.astype(F32)).astype(BF16)
    wait_for(recv.at[1], grad_t, GROUP - 1)
    grads = jnp.concatenate([grad_r[k].reshape(ROWS * TI, CH) for k in range(COLS)], axis=1)
    d_left = dot(grads, rbd[...]).astype(BF16)
    for k in range(COLS):
        dl_s[k] = d_left[:, k * CH : (k + 1) * CH].reshape(ROWS, TI, CH)
    scatter_back(dl_s, dl_r, 3)
    wait_for(recv.at[2], left_t, GROUP - 1)
    lefts = jnp.concatenate([left_r[k].reshape(ROWS * TI, CH) for k in range(COLS)], axis=1)
    d_right = dot_tn(grads, lefts)
    for k in range(COLS):
        for j in range(COLS):
            tile = d_right[j * CH : (j + 1) * CH, k * CH : (k + 1) * CH]
            dr_s[k, 4 * j : 4 * j + 4] = (
                jnp.where(low, tile[:TJ], tile[TJ:]).astype(BF16).reshape(4, TI, CH)
            )
    scatter_back(dr_s, dr_r, 4)
    sum_up(0)

    need(12, 13, 14, 15)
    w_a[:, :CH] = w_proj_a[...]
    w_a[:, CH:] = w_gate_a[...]
    w_b[:, :CH] = w_proj_b[...]
    w_b[:, CH:] = w_gate_b[...]

    def side(arr, n, sig, proj):
        wait_for(recv.at[n], right_t, GROUP - 1)
        tmp[...] = arr[...].reshape(CELLS, CH).astype(F32)

        def go(s, _):
            at, cells = pl.ds(s * STEP, STEP), pl.ds(s * SPAN, SPAN)
            out = turned([tmp[pl.ds(s * STEP + h, GROUP, stride=TI), :] for h in range(STEP)])
            dd = jnp.concatenate([out[:, h * CH : (h + 1) * CH] for h in range(STEP)], axis=0)
            sg = sig[cells, :]
            ds = dd * sg
            gpg_s[cells, :CH] = ds.astype(BF16)
            gpg_s[cells, CH:] = (ds * proj[at].reshape(SPAN, CH).astype(F32) * (1.0 - sg)).astype(BF16)
            return 0

        lax.fori_loop(0, TURNS, go, 0, unroll=TURNS)
        return dot(pn_t[...], gpg_s[...]).astype(BF16)

    z, y = r // 2, lax.rem(r, 2)
    in_plane = y * COLS + c

    def along_z(src_of, dst, n):
        def go(k, _):
            pz = lax.rem(z + alternate(8 - k), 8)
            remote(src_of(pz), dst.at[z], n, pz * 2 + y, c)
            return 0

        lax.fori_loop(1, 8, go, 0)

    def over_plane(src, dst, n):
        for k in (6, 5, 7, 4, 2, 1, 3):
            remote(src, dst.at[in_plane], n, z * 2 + lax.rem(y + k // COLS, 2), lax.rem(c + k % COLS, COLS))

    both = side(dl_r, 3, sig_a, proj_a)
    tail_p[0, 0:4] = both[:, :CH].reshape(4, 32, CH)
    tail_p[0, 4:8] = both[:, CH:].reshape(4, 32, CH)
    along_z(lambda pz: tail_p.at[0, pz], tail_z.at[0], 6)
    tail_z[0, z] = tail_p[0, z]

    def more(s, _):
        cells = pl.ds(s * SPAN, SPAN)
        gn_s[cells, :] += dot_nt(gpg_s[cells, :], w_a[...])
        return 0

    lax.fori_loop(0, TURNS, more, 0, unroll=TURNS)
    both = side(dr_r, 4, sig_b, proj_b)
    tail_p[1, 0:4] = both[:, :CH].reshape(4, 32, CH)
    tail_p[1, 4:8] = both[:, CH:].reshape(4, 32, CH)
    along_z(lambda pz: tail_p.at[1, pz], tail_z.at[1], 7)
    tail_z[1, z] = tail_p[1, z]

    def last(s, _):
        at, cells = pl.ds(s * STEP, STEP), pl.ds(s * SPAN, SPAN)
        gn = gn_s[cells, :] + dot_nt(gpg_s[cells, :], w_b[...])
        normed = normed_s[cells, :]
        vec_acc[2] += fold_rows(gn * normed)
        vec_acc[3] += fold_rows(gn)
        back = norm_back(gn * g_in, normed, inv_s[cells, :])
        pair_o[at] = back.astype(BF16).reshape(STEP, TJ, CH)
        return 0

    lax.fori_loop(0, TURNS, last, 0, unroll=TURNS)
    for n in range(4):
        vec_s[n : n + 1, :] = jnp.sum(vec_acc[n], axis=0, keepdims=True)
    for k in range(1, COLS):
        remote(vec_s, vec_r.at[c], 11, r, lax.rem(c + k, COLS))
    vec_r[c] = vec_s[...]
    wait_for(recv.at[6], tail_p.at[0], 7)
    wait_for(recv.at[7], tail_p.at[1], 7)
    tail_s[...] = jnp.sum(tail_z[...].astype(F32), axis=1).astype(BF16)
    over_plane(tail_s, tail_x, 10)
    tail_x[in_plane] = tail_s[...]
    wait_for(recv.at[11], vec_r, COLS - 1)
    vec_c[...] = jnp.sum(vec_r[...], axis=0)

    def over_rows(k, _):
        remote(vec_c, vec_a.at[r], 12, lax.rem(r + k, ROWS), c)
        return 0

    lax.fori_loop(1, ROWS, over_rows, 0)
    vec_a[r] = vec_c[...]
    wait_for(recv.at[10], tail_x, 7)
    tail_t[...] = jnp.sum(tail_x[...].astype(F32), axis=0).astype(BF16)
    along_z(lambda pz: tail_t, tail_f, 13)
    tail_f[z] = tail_t[...]
    wait_for(recv.at[12], vec_a, ROWS - 1)
    vec_o[...] = jnp.sum(vec_a[...], axis=0)
    for g, outs in ((0, (4, 5)),):
        summed(g)
        w_o[outs[0]][...] = final[g, 0:8].astype(F32).reshape(CH, CH)
        w_o[outs[1]][...] = final[g, 8:16].astype(F32).reshape(CH, CH)
    wait_for(recv.at[13], tail_x, 7)
    for n in range(4):
        w_o[n][...] = tail_f[4 * (n % 2) : 4 * (n % 2) + 4, n // 2].astype(F32).reshape(CH, CH)
    for n in range(2):
        wait_for(send.at[6 + n], tail_p.at[n], 7)
    for n in (10, 13):
        wait_for(send.at[n], tail_x, 7)
    for n in range(5):
        wait_for(send.at[n], right_t, GROUP - 1)
    sums_left(0)
    wait_for(send.at[11], vec_r, COLS - 1)
    wait_for(send.at[12], vec_a, ROWS - 1)


def hand_out(*refs):
    (pair_in, vec_in, *w_in), (pair_o, *vec_o), w_o, sem = refs[:8], refs[8:13], refs[13:19], refs[19]
    copies = [pltpu.make_async_copy(pair_in, pair_o, sem.at[0])]
    for n in range(4):
        copies.append(pltpu.make_async_copy(vec_in.at[pl.ds(n, 1)], vec_o[n], sem.at[1 + n]))
    for n in range(6):
        copies.append(pltpu.make_async_copy(w_in[n], w_o[n], sem.at[5 + n]))
    for copy in copies:
        copy.start()
    for copy in copies:
        copy.wait()


def local(
    pair_act, gain_in, bias_in, proj_a, gate_a, proj_b, gate_b, tri_out, gain_tri, bias_tri,
    gate_out, cotangent, w_proj_a, w_gate_a, w_proj_b, w_gate_b, w_out, w_gate,
):
    args = (
        pair_act, proj_a, gate_a, proj_b, gate_b, tri_out, gate_out, cotangent,
        gain_in.reshape(1, CH), bias_in.reshape(1, CH), gain_tri.reshape(1, CH), bias_tri.reshape(1, CH),
        w_proj_a, w_gate_a, w_proj_b, w_gate_b, w_out, w_gate,
    )
    hbm = pl.BlockSpec(memory_space=pltpu.HBM)
    vmem = pl.BlockSpec(memory_space=pltpu.VMEM)
    square = jax.ShapeDtypeStruct((CH, CH), F32)
    turned = pltpu.VMEM((GROUP, TI, CH), BF16)
    landed = pltpu.VMEM((COLS, ROWS, TI, CH), BF16)
    wide = pltpu.VMEM((CELLS, CH), F32)
    eight = pltpu.VMEM((8, 2, 32, CH), BF16)
    half = pltpu.VMEM((CELLS, CH), BF16)
    outs = pl.pallas_call(
        kernel,
        out_shape=(
            jax.ShapeDtypeStruct(pair_act.shape, BF16),
            jax.ShapeDtypeStruct((4, CH), F32),
            square, square, square, square, square, square,
        ),
        in_specs=[hbm] * 18,
        out_specs=tuple([vmem] * 8),
        scratch_shapes=[pltpu.VMEM(a.shape, a.dtype) for a in args] + [
            wide, wide, turned, turned, turned, landed, landed, landed,
            landed, landed, turned, turned, pltpu.VMEM((4 * CH, 4 * CH), BF16),
            wide, wide, half, half, half, wide, wide, half, pltpu.VMEM((CH, CELLS), BF16), wide,
            pltpu.VMEM((CELLS, 2 * CH), BF16), pltpu.VMEM((CH, 2 * CH), BF16), pltpu.VMEM((CH, 2 * CH), BF16),
            pltpu.VMEM((1, ROWS, 16, CH), BF16), pltpu.VMEM((1, GROUP, 16, CH), BF16),
            pltpu.VMEM((1, ROWS, 16, CH), BF16),
            pltpu.VMEM((2, 8, 32, CH), BF16), pltpu.VMEM((2, 8, 32, CH), BF16), pltpu.VMEM((2, 32, CH), BF16), eight,
            pltpu.VMEM((2, 32, CH), BF16), eight,
            pltpu.VMEM((4, 8, CH), F32),
            pltpu.VMEM((4, CH), F32), pltpu.VMEM((COLS, 4, CH), F32),
            pltpu.VMEM((4, CH), F32), pltpu.VMEM((ROWS, 4, CH), F32),
            pltpu.SemaphoreType.DMA((18,)),
            pltpu.SemaphoreType.DMA((14,)), pltpu.SemaphoreType.DMA((14,)),
        ],
        compiler_params=pltpu.CompilerParams(
            collective_id=0, has_side_effects=True, vmem_limit_bytes=63 * 1024 * 1024
        ),
        name="triangle_backward",
    )(*args)
    vector = jax.ShapeDtypeStruct((1, CH), F32)
    pair_grad, v0, v1, v2, v3, *weights = pl.pallas_call(
        hand_out,
        out_shape=(jax.ShapeDtypeStruct(pair_act.shape, BF16),) + (vector,) * 4 + (square,) * 6,
        in_specs=[vmem] * 8,
        out_specs=tuple([hbm] * 11),
        scratch_shapes=[pltpu.SemaphoreType.DMA((11,))],
        name="hand_out",
    )(*outs)
    vecs = [v.reshape(CH) for v in (v2, v3, v0, v1)]
    return (pair_grad, *vecs, *weights)


def solution(mesh):
    tile = P(("dp", "row"), "col", None)
    placed = (
        tile, P(), P(), tile, tile, tile, tile, tile, P(), P(),
        tile, tile, P(), P(), P(), P(), P(), P(),
    )
    vector, matrix = P("dp"), P("dp", None)
    return jax.shard_map(
        local,
        mesh=mesh,
        in_specs=placed,
        out_specs=(tile,) + (vector,) * 4 + (matrix,) * 6,
        check_vma=False,
    )
```

```python
import jax
import jax.numpy as jnp
from jax import lax
from jax.experimental import pallas as pl
from jax.experimental.pallas import tpu as pltpu
from jax.sharding import PartitionSpec as P

MESH = pl.DeviceIdType.MESH
F32 = jnp.float32
BF16 = jnp.bfloat16
ROWS = 16
COLS = 4
GROUP = ROWS * COLS
TI = 16
TJ = 64
CELLS = TI * TJ
CH = 128
STEP = 2
TURNS = TI // STEP
SPAN = STEP * TJ
BIG = 8


def dot(a, b):
    return jnp.dot(a, b, preferred_element_type=F32)


def dot_nt(a, b):
    return lax.dot_general(a, b, (((1,), (1,)), ((), ())), preferred_element_type=F32)


def dot_tn(a, b):
    return lax.dot_general(a, b, (((0,), (0,)), ((), ())), preferred_element_type=F32)


def sigmoid(x):
    return 1.0 / (1.0 + jnp.exp(-x))


def normalize(values):
    average = jnp.mean(values, axis=-1, keepdims=True)
    centred = values - average
    inverse = lax.rsqrt(jnp.mean(centred * centred, axis=-1, keepdims=True) + 1e-05)
    return centred * inverse, inverse


def norm_back(grad_hat, normed, inverse):
    grad_mean = jnp.mean(grad_hat, axis=-1, keepdims=True)
    grad_corr = jnp.mean(grad_hat * normed, axis=-1, keepdims=True)
    return inverse * (grad_hat - grad_mean - normed * grad_corr)


def alternate(n):
    return lax.rem(jnp.where(lax.rem(n, 2) == 1, (n + 1) // 2, 8 - n // 2), 8)


def fold_rows(x):
    return jnp.sum(x.reshape(-1, 8, CH), axis=0)


def kernel(*refs):
    hbm_in, refs = refs[:18], refs[18:]
    (pair_o, vec_o, *w_o), refs = refs[:8], refs[8:]
    held, refs = refs[:18], refs[18:]
    (pair_act, proj_a, gate_a, proj_b, gate_b, tri_out, gate_out, cotangent,
     gain_in, bias_in, gain_tri, bias_tri,
     w_proj_a, w_gate_a, w_proj_b, w_gate_b, w_out, w_gate) = held
    (tmp, tmp2, left_t, right_t, grad_t, left_r, right_r, grad_r,
     dl_s, dr_s, dl_r, dr_r, rbd,
     sig_a, sig_b, mixed_s, lift_s, ggate_s, normed_s, inv_s, pn_s, pn_t, gn_s, gpg_s, w_a, w_b,
     sum_p, sum_x, sum_s, sum_z, sum_t, sum_f, vec_acc, vec_s, vec_r, vec_c, vec_a,
     in_sem, send, recv) = refs
    d, r, c = lax.axis_index("dp"), lax.axis_index("row"), lax.axis_index("col")
    mine = r * COLS + c

    fetches = [pltpu.make_async_copy(hbm_in[n], held[n], in_sem.at[n]) for n in range(18)]
    for n in (4, 3):
        fetches[n].start()

    def need(*ns):
        for n in ns:
            fetches[n].wait()

    cols = [lax.rem(c + k, COLS) for k in range(COLS)]

    def to_peers(copy):
        def go(k, _):
            k = ROWS - k
            pr = lax.rem(r // 2 + alternate(lax.rem(k, 8)), 8) * 2 + lax.rem(lax.rem(r, 2) + k // 8, 2)
            for n in (2, 1, 3, 0):
                copy(pr, cols[n])
            return 0

        lax.fori_loop(1, ROWS, go, 0)
        for n in (2, 1, 3):
            copy(r, cols[n])

    barrier = pltpu.get_barrier_semaphore()

    def greet(pr, pc):
        pl.semaphore_signal(barrier, inc=1, device_id=(d, pr, pc), device_id_type=MESH)

    to_peers(greet)
    for n in (5, 6, 7, 16, 10, 11, 2, 1, 0, 8, 9, 17, 12, 13, 14, 15):
        fetches[n].start()

    lane = lax.broadcasted_iota(jnp.int32, (TJ, CH), 1)
    low = lane < TJ
    row = lax.broadcasted_iota(jnp.int32, (TJ, CH), 0)
    fold = jnp.where(lax.rem(lane, TJ) == row, 1.0, 0.0).astype(BF16)

    def halves(x):
        zero = jnp.zeros_like(x)
        return jnp.concatenate([jnp.where(low, x, zero), jnp.where(low, zero, x)], axis=0)

    def turned(blocks):
        return dot_nt(fold, jnp.concatenate([halves(b) for b in blocks], axis=0).astype(BF16))

    def spread(scratch, s, flat):
        out = turned([flat[h * TJ : (h + 1) * TJ] for h in range(STEP)])
        for h in range(STEP):
            scratch[pl.ds(s * STEP + h, GROUP, stride=TI), :] = out[:, h * CH : (h + 1) * CH]

    def remote(src, dst, n, pr, pc):
        pltpu.make_async_remote_copy(
            src_ref=src, dst_ref=dst, send_sem=send.at[n], recv_sem=recv.at[n],
            device_id=(d, pr, pc), device_id_type=MESH,
        ).start()

    def scatter(source, target, n):
        to_peers(lambda pr, pc: remote(source.at[pr * COLS + pc], target.at[c, r], n, pr, pc))
        target[c, r] = source[mine]

    def scatter_back(source, target, n):
        to_peers(lambda pr, pc: remote(source.at[pc, pr], target.at[mine], n, pr, pc))
        target[mine] = source[c, r]

    def wait_for(sem, like, count):
        view = like.at[pl.ds(0, count)]
        pltpu.make_async_copy(view, view, sem).wait()

    def acts(gate, proj, sig, scratch):
        def go(s, _):
            at = pl.ds(s * STEP, STEP)
            sg = sigmoid(gate[at].reshape(SPAN, CH).astype(F32))
            sig[pl.ds(s * SPAN, SPAN), :] = sg
            act = sg * proj[at].reshape(SPAN, CH).astype(F32)
            spread(scratch, s, act.astype(BF16).astype(F32))
            return 0

        lax.fori_loop(0, TURNS, go, 0, unroll=TURNS)

    need(4, 3)
    acts(gate_b, proj_b, sig_b, tmp)
    right_t[...] = tmp[...].astype(BF16).reshape(GROUP, TI, CH)

    pl.semaphore_wait(barrier, GROUP - 1)
    scatter(right_t, right_r, 0)

    need(5, 6, 7, 16, 10, 11)
    g_tri, b_tri = gain_tri[...], bias_tri[...]
    vec_acc[...] = jnp.zeros_like(vec_acc)

    def outer(s, _):
        at, cells = pl.ds(s * STEP, STEP), pl.ds(s * SPAN, SPAN)
        hat, inv = normalize(tri_out[at].reshape(SPAN, CH).astype(F32))
        mixed = (hat * g_tri + b_tri).astype(BF16)
        lifted = dot(mixed, w_out[...])
        sg = sigmoid(gate_out[at].reshape(SPAN, CH).astype(F32))
        up = cotangent[at].reshape(SPAN, CH).astype(F32)
        ups = up * sg
        lift = ups.astype(BF16)
        ggate_s[cells, :] = (ups * lifted * (1.0 - sg)).astype(BF16)
        mixed_s[cells, :] = mixed
        lift_s[cells, :] = lift
        gm = dot_nt(lift, w_out[...])
        vec_acc[0] += fold_rows(gm * hat)
        vec_acc[1] += fold_rows(gm)
        gt = norm_back(gm * g_tri, hat, inv)
        spread(tmp2, s, gt.astype(BF16).astype(F32))
        return 0

    lax.fori_loop(0, TURNS, outer, 0, unroll=TURNS)
    grad_t[...] = tmp2[...].astype(BF16).reshape(GROUP, TI, CH)

    scatter(grad_t, grad_r, 1)

    need(2, 1)
    acts(gate_a, proj_a, sig_a, tmp)
    left_t[...] = tmp[...].astype(BF16).reshape(GROUP, TI, CH)
    scatter(left_t, left_r, 2)

    z, y = r // 2, lax.rem(r, 2)
    in_plane = y * COLS + c

    def along_z(src_of, dst, n):
        def go(k, _):
            pz = lax.rem(z + alternate(8 - k), 8)
            remote(src_of(pz), dst.at[z], n, pz * 2 + y, c)
            return 0

        lax.fori_loop(1, 8, go, 0)

    def over_plane(src_of, dst, n):
        for k in (6, 5, 7, 4, 2, 1, 3):
            py, pc = lax.rem(y + k // COLS, 2), cols[k % COLS]
            remote(src_of(py * COLS + pc), dst.at[in_plane], n, z * 2 + py, pc)

    def place(g, top, bottom):
        sum_p[g, 0:4] = top.astype(BF16).reshape(4, 32, CH)
        sum_p[g, 4:8] = bottom.astype(BF16).reshape(4, 32, CH)
        over_plane(lambda p: sum_p.at[g, p], sum_x.at[g], 5 + g)
        sum_x[g, in_plane] = sum_p[g, in_plane]

    def cross(g):
        wait_for(recv.at[5 + g], sum_p.at[g], 7)
        sum_s[g] = jnp.sum(sum_x[g].astype(F32), axis=0).astype(BF16)
        along_z(lambda pz: sum_s.at[g], sum_z.at[g], 8 + g)
        sum_z[g, z] = sum_s[g]

    def share(g):
        wait_for(recv.at[8 + g], sum_p.at[g], 7)
        sum_t[g] = jnp.sum(sum_z[g].astype(F32), axis=0).astype(BF16)
        over_plane(lambda p: sum_t.at[g], sum_f.at[g], 13 + g)
        sum_f[g, in_plane] = sum_t[g]

    def finish(g, top, bottom):
        wait_for(recv.at[13 + g], sum_p.at[g], 7)
        top[...] = sum_f[g, 0:4].astype(F32).reshape(CH, CH)
        bottom[...] = sum_f[g, 4:8].astype(F32).reshape(CH, CH)

    need(0, 8, 9, 17)
    g_in, b_in = gain_in[...], bias_in[...]

    def first(s, _):
        at, cells = pl.ds(s * STEP, STEP), pl.ds(s * SPAN, SPAN)
        normed, inv = normalize(pair_act[at].reshape(SPAN, CH).astype(F32))
        normed_s[cells, :] = normed
        inv_s[cells, :] = jnp.broadcast_to(inv, (SPAN, CH))
        pn = (normed * g_in + b_in).astype(BF16)
        pn_s[cells, :] = pn
        gn_s[cells, :] = dot_nt(ggate_s[cells, :], w_gate[...])
        return 0

    lax.fori_loop(0, TURNS, first, 0, unroll=TURNS)
    pn_t[...] = pn_s[...].astype(F32).T.astype(BF16)
    place(0, dot_tn(mixed_s[...], lift_s[...]), dot(pn_t[...], ggate_s[...]))

    wait_for(recv.at[0], right_t, GROUP - 1)
    for k in range(COLS):
        for j in range(COLS):
            tile = right_r[k, 4 * j : 4 * j + 4].reshape(TJ, CH)
            rbd[j * CH : (j + 1) * CH, k * CH : (k + 1) * CH] = halves(tile.astype(F32)).astype(BF16)
    wait_for(recv.at[1], grad_t, GROUP - 1)
    grads = jnp.concatenate([grad_r[k].reshape(ROWS * TI, CH) for k in range(COLS)], axis=1)
    d_left = dot(grads, rbd[...]).astype(BF16)
    for k in range(COLS):
        dl_s[k] = d_left[:, k * CH : (k + 1) * CH].reshape(ROWS, TI, CH)
    scatter_back(dl_s, dl_r, 3)
    cross(0)
    wait_for(recv.at[2], left_t, GROUP - 1)
    lefts = jnp.concatenate([left_r[k].reshape(ROWS * TI, CH) for k in range(COLS)], axis=1)
    d_right = dot_tn(grads, lefts)
    for k in range(COLS):
        for j in range(COLS):
            tile = d_right[j * CH : (j + 1) * CH, k * CH : (k + 1) * CH]
            dr_s[k, 4 * j : 4 * j + 4] = (
                jnp.where(low, tile[:TJ], tile[TJ:]).astype(BF16).reshape(4, TI, CH)
            )
    scatter_back(dr_s, dr_r, 4)
    share(0)

    need(12, 13, 14, 15)
    w_a[:, :CH] = w_proj_a[...]
    w_a[:, CH:] = w_gate_a[...]
    w_b[:, :CH] = w_proj_b[...]
    w_b[:, CH:] = w_gate_b[...]

    def side(arr, n, sig, proj):
        wait_for(recv.at[n], right_t, GROUP - 1)
        tmp[...] = arr[...].reshape(CELLS, CH).astype(F32)

        def go(s, _):
            at, cells = pl.ds(s * STEP, STEP), pl.ds(s * SPAN, SPAN)
            out = turned([tmp[pl.ds(s * STEP + h, GROUP, stride=TI), :] for h in range(STEP)])
            dd = jnp.concatenate([out[:, h * CH : (h + 1) * CH] for h in range(STEP)], axis=0)
            sg = sig[cells, :]
            ds = dd * sg
            gpg_s[cells, :CH] = ds.astype(BF16)
            gpg_s[cells, CH:] = (ds * proj[at].reshape(SPAN, CH).astype(F32) * (1.0 - sg)).astype(BF16)
            return 0

        lax.fori_loop(0, TURNS, go, 0, unroll=TURNS)
        return dot(pn_t[...], gpg_s[...])

    both = side(dl_r, 3, sig_a, proj_a)
    place(1, both[:, :CH], both[:, CH:])

    def more(s, _):
        cells = pl.ds(s * SPAN, SPAN)
        gn_s[cells, :] += dot_nt(gpg_s[cells, :], w_a[...])
        return 0

    lax.fori_loop(0, TURNS, more, 0, unroll=TURNS)
    both = side(dr_r, 4, sig_b, proj_b)
    place(2, both[:, :CH], both[:, CH:])

    def last(s, _):
        at, cells = pl.ds(s * STEP, STEP), pl.ds(s * SPAN, SPAN)
        gn = gn_s[cells, :] + dot_nt(gpg_s[cells, :], w_b[...])
        normed = normed_s[cells, :]
        vec_acc[2] += fold_rows(gn * normed)
        vec_acc[3] += fold_rows(gn)
        back = norm_back(gn * g_in, normed, inv_s[cells, :])
        pair_o[at] = back.astype(BF16).reshape(STEP, TJ, CH)
        return 0

    lax.fori_loop(0, TURNS, last, 0, unroll=TURNS)
    for n in range(4):
        vec_s[n : n + 1, :] = jnp.sum(vec_acc[n], axis=0, keepdims=True)
    for k in range(1, COLS):
        remote(vec_s, vec_r.at[c], 11, r, lax.rem(c + k, COLS))
    vec_r[c] = vec_s[...]
    cross(1)
    cross(2)
    wait_for(recv.at[11], vec_r, COLS - 1)
    vec_c[...] = jnp.sum(vec_r[...], axis=0)

    def over_rows(k, _):
        remote(vec_c, vec_a.at[r], 12, lax.rem(r + k, ROWS), c)
        return 0

    lax.fori_loop(1, ROWS, over_rows, 0)
    vec_a[r] = vec_c[...]
    share(1)
    share(2)
    wait_for(recv.at[12], vec_a, ROWS - 1)
    vec_o[...] = jnp.sum(vec_a[...], axis=0)
    finish(0, w_o[4], w_o[5])
    finish(1, w_o[0], w_o[1])
    finish(2, w_o[2], w_o[3])
    for g in range(3):
        for n in (5, 8, 13):
            wait_for(send.at[n + g], sum_p.at[g], 7)
    for n in range(5):
        wait_for(send.at[n], right_t, GROUP - 1)
    wait_for(send.at[11], vec_r, COLS - 1)
    wait_for(send.at[12], vec_a, ROWS - 1)


def hand_out(*refs):
    (pair_in, vec_in, *w_in), (pair_o, *vec_o), w_o, sem = refs[:8], refs[8:13], refs[13:19], refs[19]
    copies = [pltpu.make_async_copy(pair_in, pair_o, sem.at[0])]
    for n in range(4):
        copies.append(pltpu.make_async_copy(vec_in.at[pl.ds(n, 1)], vec_o[n], sem.at[1 + n]))
    for n in range(6):
        copies.append(pltpu.make_async_copy(w_in[n], w_o[n], sem.at[5 + n]))
    for copy in copies:
        copy.start()
    for copy in copies:
        copy.wait()


def local(
    pair_act, gain_in, bias_in, proj_a, gate_a, proj_b, gate_b, tri_out, gain_tri, bias_tri,
    gate_out, cotangent, w_proj_a, w_gate_a, w_proj_b, w_gate_b, w_out, w_gate,
):
    args = (
        pair_act, proj_a, gate_a, proj_b, gate_b, tri_out, gate_out, cotangent,
        gain_in.reshape(1, CH), bias_in.reshape(1, CH), gain_tri.reshape(1, CH), bias_tri.reshape(1, CH),
        w_proj_a, w_gate_a, w_proj_b, w_gate_b, w_out, w_gate,
    )
    hbm = pl.BlockSpec(memory_space=pltpu.HBM)
    vmem = pl.BlockSpec(memory_space=pltpu.VMEM)
    square = jax.ShapeDtypeStruct((CH, CH), F32)
    turned = pltpu.VMEM((GROUP, TI, CH), BF16)
    landed = pltpu.VMEM((COLS, ROWS, TI, CH), BF16)
    wide = pltpu.VMEM((CELLS, CH), F32)
    eight = pltpu.VMEM((3, 8, 32, CH), BF16)
    one = pltpu.VMEM((3, 32, CH), BF16)
    half = pltpu.VMEM((CELLS, CH), BF16)
    outs = pl.pallas_call(
        kernel,
        out_shape=(
            jax.ShapeDtypeStruct(pair_act.shape, BF16),
            jax.ShapeDtypeStruct((4, CH), F32),
            square, square, square, square, square, square,
        ),
        in_specs=[hbm] * 18,
        out_specs=tuple([vmem] * 8),
        scratch_shapes=[pltpu.VMEM(a.shape, a.dtype) for a in args] + [
            wide, wide, turned, turned, turned, landed, landed, landed,
            landed, landed, turned, turned, pltpu.VMEM((4 * CH, 4 * CH), BF16),
            wide, wide, half, half, half, wide, wide, half, pltpu.VMEM((CH, CELLS), BF16), wide,
            pltpu.VMEM((CELLS, 2 * CH), BF16), pltpu.VMEM((CH, 2 * CH), BF16), pltpu.VMEM((CH, 2 * CH), BF16),
            eight, eight, one, eight, one, eight,
            pltpu.VMEM((4, 8, CH), F32),
            pltpu.VMEM((4, CH), F32), pltpu.VMEM((COLS, 4, CH), F32),
            pltpu.VMEM((4, CH), F32), pltpu.VMEM((ROWS, 4, CH), F32),
            pltpu.SemaphoreType.DMA((18,)),
            pltpu.SemaphoreType.DMA((16,)), pltpu.SemaphoreType.DMA((16,)),
        ],
        compiler_params=pltpu.CompilerParams(
            collective_id=0, has_side_effects=True, vmem_limit_bytes=63 * 1024 * 1024
        ),
        name="triangle_backward",
    )(*args)
    vector = jax.ShapeDtypeStruct((1, CH), F32)
    pair_grad, v0, v1, v2, v3, *weights = pl.pallas_call(
        hand_out,
        out_shape=(jax.ShapeDtypeStruct(pair_act.shape, BF16),) + (vector,) * 4 + (square,) * 6,
        in_specs=[vmem] * 8,
        out_specs=tuple([hbm] * 11),
        scratch_shapes=[pltpu.SemaphoreType.DMA((11,))],
        name="hand_out",
    )(*outs)
    vecs = [v.reshape(CH) for v in (v2, v3, v0, v1)]
    return (pair_grad, *vecs, *weights)


def solution(mesh):
    tile = P(("dp", "row"), "col", None)
    placed = (
        tile, P(), P(), tile, tile, tile, tile, tile, P(), P(),
        tile, tile, P(), P(), P(), P(), P(), P(),
    )
    vector, matrix = P("dp"), P("dp", None)
    return jax.shard_map(
        local,
        mesh=mesh,
        in_specs=placed,
        out_specs=(tile,) + (vector,) * 4 + (matrix,) * 6,
        check_vma=False,
    )
```

```python
import jax
import jax.numpy as jnp
from jax import lax
from jax.experimental import pallas as pl
from jax.experimental.pallas import tpu as pltpu
from jax.sharding import PartitionSpec as P

MESH = pl.DeviceIdType.MESH
F32 = jnp.float32
BF16 = jnp.bfloat16
ROWS = 16
COLS = 4
GROUP = ROWS * COLS
TI = 16
TJ = 64
CELLS = TI * TJ
CH = 128
STEP = 2
TURNS = TI // STEP
SPAN = STEP * TJ
BIG = 8


def dot(a, b):
    return jnp.dot(a, b, preferred_element_type=F32)


def dot_nt(a, b):
    return lax.dot_general(a, b, (((1,), (1,)), ((), ())), preferred_element_type=F32)


def dot_tn(a, b):
    return lax.dot_general(a, b, (((0,), (0,)), ((), ())), preferred_element_type=F32)


def sigmoid(x):
    return 1.0 / (1.0 + jnp.exp(-x))


def normalize(values):
    average = jnp.mean(values, axis=-1, keepdims=True)
    centred = values - average
    inverse = lax.rsqrt(jnp.mean(centred * centred, axis=-1, keepdims=True) + 1e-05)
    return centred * inverse, inverse


def norm_back(grad_hat, normed, inverse):
    grad_mean = jnp.mean(grad_hat, axis=-1, keepdims=True)
    grad_corr = jnp.mean(grad_hat * normed, axis=-1, keepdims=True)
    return inverse * (grad_hat - grad_mean - normed * grad_corr)


def alternate(n):
    return lax.rem(jnp.where(lax.rem(n, 2) == 1, (n + 1) // 2, 8 - n // 2), 8)


def fold_rows(x):
    return jnp.sum(x.reshape(-1, 8, CH), axis=0)


def kernel(*refs):
    hbm_in, refs = refs[:18], refs[18:]
    (pair_o, vec_o, *w_o), refs = refs[:8], refs[8:]
    held, refs = refs[:18], refs[18:]
    (pair_act, proj_a, gate_a, proj_b, gate_b, tri_out, gate_out, cotangent,
     gain_in, bias_in, gain_tri, bias_tri,
     w_proj_a, w_gate_a, w_proj_b, w_gate_b, w_out, w_gate) = held
    (tmp, tmp2, left_t, right_t, grad_t, left_r, right_r, grad_r,
     dl_s, dr_s, dl_r, dr_r, rbd,
     sig_a, sig_b, mixed_s, lift_s, ggate_s, normed_s, inv_s, pn_s, pn_t, gn_s, gpg_s, w_a, w_b,
     sum_p, sum_x, sum_s, sum_z, sum_t, sum_f, vec_acc, vec_s, vec_r, vec_c, vec_a,
     in_sem, send, recv) = refs
    d, r, c = lax.axis_index("dp"), lax.axis_index("row"), lax.axis_index("col")
    mine = r * COLS + c

    fetches = [pltpu.make_async_copy(hbm_in[n], held[n], in_sem.at[n]) for n in range(18)]
    first_half = []
    for q in range(2):
        piece = pl.ds(q * TI // 2, TI // 2)
        for n in (4, 3):
            first_half.append(pltpu.make_async_copy(hbm_in[n].at[piece], held[n].at[piece], in_sem.at[n if q == 0 else n + 15]))
    for copy in first_half:
        copy.start()

    def need(*ns):
        for n in ns:
            fetches[n].wait()

    cols = [lax.rem(c + k, COLS) for k in range(COLS)]

    def to_peers(copy):
        def go(k, _):
            k = ROWS - k
            pr = lax.rem(r // 2 + alternate(lax.rem(k, 8)), 8) * 2 + lax.rem(lax.rem(r, 2) + k // 8, 2)
            for n in (2, 1, 3, 0):
                copy(pr, cols[n])
            return 0

        lax.fori_loop(1, ROWS, go, 0)
        for n in (2, 1, 3):
            copy(r, cols[n])

    barrier = pltpu.get_barrier_semaphore()

    def greet(pr, pc):
        pl.semaphore_signal(barrier, inc=1, device_id=(d, pr, pc), device_id_type=MESH)

    to_peers(greet)
    for n in (5, 6, 7, 16, 10, 11, 2, 1, 0, 8, 9, 17, 12, 13, 14, 15):
        fetches[n].start()

    lane = lax.broadcasted_iota(jnp.int32, (TJ, CH), 1)
    low = lane < TJ
    row = lax.broadcasted_iota(jnp.int32, (TJ, CH), 0)
    fold = jnp.where(lax.rem(lane, TJ) == row, 1.0, 0.0).astype(BF16)

    def halves(x):
        zero = jnp.zeros_like(x)
        return jnp.concatenate([jnp.where(low, x, zero), jnp.where(low, zero, x)], axis=0)

    def turned(blocks):
        return dot_nt(fold, jnp.concatenate([halves(b) for b in blocks], axis=0).astype(BF16))

    def spread(scratch, s, flat):
        out = turned([flat[h * TJ : (h + 1) * TJ] for h in range(STEP)])
        for h in range(STEP):
            scratch[pl.ds(s * STEP + h, GROUP, stride=TI), :] = out[:, h * CH : (h + 1) * CH]

    def remote(src, dst, n, pr, pc):
        pltpu.make_async_remote_copy(
            src_ref=src, dst_ref=dst, send_sem=send.at[n], recv_sem=recv.at[n],
            device_id=(d, pr, pc), device_id_type=MESH,
        ).start()

    def scatter(source, target, n):
        to_peers(lambda pr, pc: remote(source.at[pr * COLS + pc], target.at[c, r], n, pr, pc))
        target[c, r] = source[mine]

    def scatter_back(source, target, n):
        to_peers(lambda pr, pc: remote(source.at[pc, pr], target.at[mine], n, pr, pc))
        target[mine] = source[c, r]

    def wait_for(sem, like, count):
        view = like.at[pl.ds(0, count)]
        pltpu.make_async_copy(view, view, sem).wait()

    def acts(gate, proj, sig, scratch, begin=0, end=TURNS):
        def go(s, _):
            at = pl.ds(s * STEP, STEP)
            sg = sigmoid(gate[at].reshape(SPAN, CH).astype(F32))
            sig[pl.ds(s * SPAN, SPAN), :] = sg
            act = sg * proj[at].reshape(SPAN, CH).astype(F32)
            spread(scratch, s, act.astype(BF16).astype(F32))
            return 0

        lax.fori_loop(begin, end, go, 0, unroll=end - begin)

    for q in range(2):
        for copy in first_half[2 * q : 2 * q + 2]:
            copy.wait()
        acts(gate_b, proj_b, sig_b, tmp, q * TURNS // 2, (q + 1) * TURNS // 2)
    right_t[...] = tmp[...].astype(BF16).reshape(GROUP, TI, CH)

    pl.semaphore_wait(barrier, GROUP - 1)
    scatter(right_t, right_r, 0)

    need(5, 6, 7, 16, 10, 11)
    g_tri, b_tri = gain_tri[...], bias_tri[...]
    vec_acc[...] = jnp.zeros_like(vec_acc)

    def outer(s, _):
        at, cells = pl.ds(s * STEP, STEP), pl.ds(s * SPAN, SPAN)
        hat, inv = normalize(tri_out[at].reshape(SPAN, CH).astype(F32))
        mixed = (hat * g_tri + b_tri).astype(BF16)
        lifted = dot(mixed, w_out[...])
        sg = sigmoid(gate_out[at].reshape(SPAN, CH).astype(F32))
        up = cotangent[at].reshape(SPAN, CH).astype(F32)
        ups = up * sg
        lift = ups.astype(BF16)
        ggate_s[cells, :] = (ups * lifted * (1.0 - sg)).astype(BF16)
        mixed_s[cells, :] = mixed
        lift_s[cells, :] = lift
        gm = dot_nt(lift, w_out[...])
        vec_acc[0] += fold_rows(gm * hat)
        vec_acc[1] += fold_rows(gm)
        gt = norm_back(gm * g_tri, hat, inv)
        spread(tmp2, s, gt.astype(BF16).astype(F32))
        return 0

    lax.fori_loop(0, TURNS, outer, 0, unroll=TURNS)
    grad_t[...] = tmp2[...].astype(BF16).reshape(GROUP, TI, CH)

    scatter(grad_t, grad_r, 1)

    need(2, 1)
    acts(gate_a, proj_a, sig_a, tmp)
    left_t[...] = tmp[...].astype(BF16).reshape(GROUP, TI, CH)
    scatter(left_t, left_r, 2)

    z, y = r // 2, lax.rem(r, 2)
    in_plane = y * COLS + c

    def along_z(src_of, dst, n):
        def go(k, _):
            pz = lax.rem(z + alternate(8 - k), 8)
            remote(src_of(pz), dst.at[z], n, pz * 2 + y, c)
            return 0

        lax.fori_loop(1, 8, go, 0)

    def over_plane(src_of, dst, n):
        for k in (6, 5, 7, 4, 2, 1, 3):
            py, pc = lax.rem(y + k // COLS, 2), cols[k % COLS]
            remote(src_of(py * COLS + pc), dst.at[in_plane], n, z * 2 + py, pc)

    def place(g, top, bottom):
        sum_p[g, 0:4] = top.astype(BF16).reshape(4, 32, CH)
        sum_p[g, 4:8] = bottom.astype(BF16).reshape(4, 32, CH)
        over_plane(lambda p: sum_p.at[g, p], sum_x.at[g], 5 + g)
        sum_x[g, in_plane] = sum_p[g, in_plane]

    def cross(g):
        wait_for(recv.at[5 + g], sum_p.at[g], 7)
        sum_s[g] = jnp.sum(sum_x[g].astype(F32), axis=0).astype(BF16)
        along_z(lambda pz: sum_s.at[g], sum_z.at[g], 8 + g)
        sum_z[g, z] = sum_s[g]

    def share(g):
        wait_for(recv.at[8 + g], sum_p.at[g], 7)
        sum_t[g] = jnp.sum(sum_z[g].astype(F32), axis=0).astype(BF16)
        over_plane(lambda p: sum_t.at[g], sum_f.at[g], 13 + g)
        sum_f[g, in_plane] = sum_t[g]

    def finish(g, top, bottom):
        wait_for(recv.at[13 + g], sum_p.at[g], 7)
        top[...] = sum_f[g, 0:4].astype(F32).reshape(CH, CH)
        bottom[...] = sum_f[g, 4:8].astype(F32).reshape(CH, CH)

    need(0, 8, 9, 17)
    g_in, b_in = gain_in[...], bias_in[...]

    def first(s, _):
        at, cells = pl.ds(s * STEP, STEP), pl.ds(s * SPAN, SPAN)
        normed, inv = normalize(pair_act[at].reshape(SPAN, CH).astype(F32))
        normed_s[cells, :] = normed
        inv_s[cells, :] = jnp.broadcast_to(inv, (SPAN, CH))
        pn = (normed * g_in + b_in).astype(BF16)
        pn_s[cells, :] = pn
        gn_s[cells, :] = dot_nt(ggate_s[cells, :], w_gate[...])
        return 0

    lax.fori_loop(0, TURNS, first, 0, unroll=TURNS)
    pn_t[...] = pn_s[...].astype(F32).T.astype(BF16)
    place(0, dot_tn(mixed_s[...], lift_s[...]), dot(pn_t[...], ggate_s[...]))

    wait_for(recv.at[0], right_t, GROUP - 1)
    for k in range(COLS):
        for j in range(COLS):
            tile = right_r[k, 4 * j : 4 * j + 4].reshape(TJ, CH)
            rbd[j * CH : (j + 1) * CH, k * CH : (k + 1) * CH] = halves(tile.astype(F32)).astype(BF16)
    wait_for(recv.at[1], grad_t, GROUP - 1)
    grads = jnp.concatenate([grad_r[k].reshape(ROWS * TI, CH) for k in range(COLS)], axis=1)
    d_left = dot(grads, rbd[...]).astype(BF16)
    for k in range(COLS):
        dl_s[k] = d_left[:, k * CH : (k + 1) * CH].reshape(ROWS, TI, CH)
    scatter_back(dl_s, dl_r, 3)
    cross(0)
    wait_for(recv.at[2], left_t, GROUP - 1)
    lefts = jnp.concatenate([left_r[k].reshape(ROWS * TI, CH) for k in range(COLS)], axis=1)
    d_right = dot_tn(grads, lefts)
    for k in range(COLS):
        for j in range(COLS):
            tile = d_right[j * CH : (j + 1) * CH, k * CH : (k + 1) * CH]
            dr_s[k, 4 * j : 4 * j + 4] = (
                jnp.where(low, tile[:TJ], tile[TJ:]).astype(BF16).reshape(4, TI, CH)
            )
    scatter_back(dr_s, dr_r, 4)
    share(0)

    need(12, 13, 14, 15)
    w_a[:, :CH] = w_proj_a[...]
    w_a[:, CH:] = w_gate_a[...]
    w_b[:, :CH] = w_proj_b[...]
    w_b[:, CH:] = w_gate_b[...]

    def side(arr, n, sig, proj):
        wait_for(recv.at[n], right_t, GROUP - 1)
        tmp[...] = arr[...].reshape(CELLS, CH).astype(F32)

        def go(s, _):
            at, cells = pl.ds(s * STEP, STEP), pl.ds(s * SPAN, SPAN)
            out = turned([tmp[pl.ds(s * STEP + h, GROUP, stride=TI), :] for h in range(STEP)])
            dd = jnp.concatenate([out[:, h * CH : (h + 1) * CH] for h in range(STEP)], axis=0)
            sg = sig[cells, :]
            ds = dd * sg
            gpg_s[cells, :CH] = ds.astype(BF16)
            gpg_s[cells, CH:] = (ds * proj[at].reshape(SPAN, CH).astype(F32) * (1.0 - sg)).astype(BF16)
            return 0

        lax.fori_loop(0, TURNS, go, 0, unroll=TURNS)
        return dot(pn_t[...], gpg_s[...])

    both = side(dl_r, 3, sig_a, proj_a)
    place(1, both[:, :CH], both[:, CH:])

    def more(s, _):
        cells = pl.ds(s * SPAN, SPAN)
        gn_s[cells, :] += dot_nt(gpg_s[cells, :], w_a[...])
        return 0

    lax.fori_loop(0, TURNS, more, 0, unroll=TURNS)
    both = side(dr_r, 4, sig_b, proj_b)
    place(2, both[:, :CH], both[:, CH:])

    def last(s, _):
        at, cells = pl.ds(s * STEP, STEP), pl.ds(s * SPAN, SPAN)
        gn = gn_s[cells, :] + dot_nt(gpg_s[cells, :], w_b[...])
        normed = normed_s[cells, :]
        vec_acc[2] += fold_rows(gn * normed)
        vec_acc[3] += fold_rows(gn)
        back = norm_back(gn * g_in, normed, inv_s[cells, :])
        pair_o[at] = back.astype(BF16).reshape(STEP, TJ, CH)
        return 0

    lax.fori_loop(0, TURNS, last, 0, unroll=TURNS)
    for n in range(4):
        vec_s[n : n + 1, :] = jnp.sum(vec_acc[n], axis=0, keepdims=True)
    for k in range(1, COLS):
        remote(vec_s, vec_r.at[c], 11, r, lax.rem(c + k, COLS))
    vec_r[c] = vec_s[...]
    cross(1)
    cross(2)
    wait_for(recv.at[11], vec_r, COLS - 1)
    vec_c[...] = jnp.sum(vec_r[...], axis=0)

    def over_rows(k, _):
        remote(vec_c, vec_a.at[r], 12, lax.rem(r + k, ROWS), c)
        return 0

    lax.fori_loop(1, ROWS, over_rows, 0)
    vec_a[r] = vec_c[...]
    share(1)
    share(2)
    wait_for(recv.at[12], vec_a, ROWS - 1)
    vec_o[...] = jnp.sum(vec_a[...], axis=0)
    finish(0, w_o[4], w_o[5])
    finish(1, w_o[0], w_o[1])
    finish(2, w_o[2], w_o[3])
    for g in range(3):
        for n in (5, 8, 13):
            wait_for(send.at[n + g], sum_p.at[g], 7)
    for n in range(5):
        wait_for(send.at[n], right_t, GROUP - 1)
    wait_for(send.at[11], vec_r, COLS - 1)
    wait_for(send.at[12], vec_a, ROWS - 1)


def hand_out(*refs):
    (pair_in, vec_in, *w_in), (pair_o, *vec_o), w_o, sem = refs[:8], refs[8:13], refs[13:19], refs[19]
    copies = [pltpu.make_async_copy(pair_in, pair_o, sem.at[0])]
    for n in range(4):
        copies.append(pltpu.make_async_copy(vec_in.at[pl.ds(n, 1)], vec_o[n], sem.at[1 + n]))
    for n in range(6):
        copies.append(pltpu.make_async_copy(w_in[n], w_o[n], sem.at[5 + n]))
    for copy in copies:
        copy.start()
    for copy in copies:
        copy.wait()


def local(
    pair_act, gain_in, bias_in, proj_a, gate_a, proj_b, gate_b, tri_out, gain_tri, bias_tri,
    gate_out, cotangent, w_proj_a, w_gate_a, w_proj_b, w_gate_b, w_out, w_gate,
):
    args = (
        pair_act, proj_a, gate_a, proj_b, gate_b, tri_out, gate_out, cotangent,
        gain_in.reshape(1, CH), bias_in.reshape(1, CH), gain_tri.reshape(1, CH), bias_tri.reshape(1, CH),
        w_proj_a, w_gate_a, w_proj_b, w_gate_b, w_out, w_gate,
    )
    hbm = pl.BlockSpec(memory_space=pltpu.HBM)
    vmem = pl.BlockSpec(memory_space=pltpu.VMEM)
    square = jax.ShapeDtypeStruct((CH, CH), F32)
    turned = pltpu.VMEM((GROUP, TI, CH), BF16)
    landed = pltpu.VMEM((COLS, ROWS, TI, CH), BF16)
    wide = pltpu.VMEM((CELLS, CH), F32)
    eight = pltpu.VMEM((3, 8, 32, CH), BF16)
    one = pltpu.VMEM((3, 32, CH), BF16)
    half = pltpu.VMEM((CELLS, CH), BF16)
    outs = pl.pallas_call(
        kernel,
        out_shape=(
            jax.ShapeDtypeStruct(pair_act.shape, BF16),
            jax.ShapeDtypeStruct((4, CH), F32),
            square, square, square, square, square, square,
        ),
        in_specs=[hbm] * 18,
        out_specs=tuple([vmem] * 8),
        scratch_shapes=[pltpu.VMEM(a.shape, a.dtype) for a in args] + [
            wide, wide, turned, turned, turned, landed, landed, landed,
            landed, landed, turned, turned, pltpu.VMEM((4 * CH, 4 * CH), BF16),
            wide, wide, half, half, half, wide, wide, half, pltpu.VMEM((CH, CELLS), BF16), wide,
            pltpu.VMEM((CELLS, 2 * CH), BF16), pltpu.VMEM((CH, 2 * CH), BF16), pltpu.VMEM((CH, 2 * CH), BF16),
            eight, eight, one, eight, one, eight,
            pltpu.VMEM((4, 8, CH), F32),
            pltpu.VMEM((4, CH), F32), pltpu.VMEM((COLS, 4, CH), F32),
            pltpu.VMEM((4, CH), F32), pltpu.VMEM((ROWS, 4, CH), F32),
            pltpu.SemaphoreType.DMA((20,)),
            pltpu.SemaphoreType.DMA((16,)), pltpu.SemaphoreType.DMA((16,)),
        ],
        compiler_params=pltpu.CompilerParams(
            collective_id=0, has_side_effects=True, vmem_limit_bytes=63 * 1024 * 1024
        ),
        name="triangle_backward",
    )(*args)
    vector = jax.ShapeDtypeStruct((1, CH), F32)
    pair_grad, v0, v1, v2, v3, *weights = pl.pallas_call(
        hand_out,
        out_shape=(jax.ShapeDtypeStruct(pair_act.shape, BF16),) + (vector,) * 4 + (square,) * 6,
        in_specs=[vmem] * 8,
        out_specs=tuple([hbm] * 11),
        scratch_shapes=[pltpu.SemaphoreType.DMA((11,))],
        name="hand_out",
    )(*outs)
    vecs = [v.reshape(CH) for v in (v2, v3, v0, v1)]
    return (pair_grad, *vecs, *weights)


def solution(mesh):
    tile = P(("dp", "row"), "col", None)
    placed = (
        tile, P(), P(), tile, tile, tile, tile, tile, P(), P(),
        tile, tile, P(), P(), P(), P(), P(), P(),
    )
    vector, matrix = P("dp"), P("dp", None)
    return jax.shard_map(
        local,
        mesh=mesh,
        in_specs=placed,
        out_specs=(tile,) + (vector,) * 4 + (matrix,) * 6,
        check_vma=False,
    )
```
